256 devices in a mesh: dp: 128 (over z, x, y), pair: 2 (over core).
Axes of the slice: x: 4, y: 4, z: 8, core: 2. Of those that a mesh axis runs over, the one named last changes fastest.
Arguments:
- hidden_in: bfloat16 [32768, 1536], P(('dp', 'pair')), may hold values from -24 to 24
- segment_ids: int32 [32768], replicated, may hold values from 0 to 511, as said below
- frame_mask: int32 [32768], P(('dp', 'pair')), may hold values from 0 to 1, as said below
- dw_kernel: float32 [31, 1536], P(None, ('dp', 'pair')), may hold values from -1 to 1
- norm_scale: float32 [1536], P(('dp', 'pair')), may hold values from 0.1 to 1.9
- norm_shift: float32 [1536], P(('dp', 'pair')), may hold values from -3 to 3
- out_weight: bfloat16 [1536, 1536], P(('dp', 'pair')), may hold values from -0.15625 to 0.15625
- cotangent: bfloat16 [32768, 1536], P(('dp', 'pair')), may hold values from -6 to 6
Outputs:
- module_out: bfloat16 [32768, 1536], P(('dp', 'pair'))
- grad_hidden: bfloat16 [32768, 1536], P(('dp', 'pair'))
- grad_kernel: float32 [31, 1536], P(None, ('dp', 'pair'))
- grad_scale: float32 [1536], P(('dp', 'pair'))
- grad_shift: float32 [1536], P(('dp', 'pair'))
- grad_weight: float32 [1536, 1536], P(('dp', 'pair'))
The draws below stay inside these ranges and needn't reach their ends.
Inputs may be any that keep to these rules, and one draw needn't show every extreme that they name: `segment_ids`: non-falling along the stream, starting at 0; each utterance has 1 to 192 frames; no utterance begins at a frame whose index is a positive multiple of 128. `frame_mask`: 1 on every frame whose index modulo 16 is 0 or 15.
All inputs are finite; a program needn't handle non-finite values.
Results may differ from the reference program's by a relative error of at most 0.0049.
Values may be sent and summed in bfloat16 or wider, within the bound.
No kernel may reach another device: no remote copies, remote signals or barrier semaphores. Data moves between devices by JAX's collectives and lax.ppermute only.
A program may use at most 128 MiB of HBM per device.

```python
import jax
import jax.numpy as jnp
from jax import lax

D = 1536
KERNEL = 31
TOK_DEV = 128
FRAMES = 32768
N_DP = 128
N_PAIR = 2


def draw_segment_ids(key, part):
    blocks_all = N_DP * N_PAIR
    position = jnp.arange(FRAMES, dtype=jnp.int32)
    owner = position // TOK_DEV
    inside = position % TOK_DEV
    middle = TOK_DEV // 2
    extra = jax.random.randint(key, (blocks_all,), 1, TOK_DEV - 2, dtype=jnp.int32)
    extra = jnp.where(extra >= middle, extra + 1, extra)
    extra_here = jnp.take(extra, owner)
    forced = (inside == middle) & (owner >= 1)
    chosen = (inside == extra_here) & (owner >= 2)
    starts = (forced | chosen) & (position > 0)
    return jnp.cumsum(starts.astype(jnp.int32)).astype(jnp.int32)


def draw_frame_mask(key, part):
    devices_all = N_DP * N_PAIR
    position = jnp.arange(FRAMES, dtype=jnp.int32)
    owner = position // TOK_DEV
    rolled = jax.random.randint(key, (FRAMES,), 0, 3 * devices_all, dtype=jnp.int32)
    keep = (rolled < devices_all + 2 * owner) | (position % 16 == 0) | (position % 16 == 15)
    return keep.astype(jnp.int32)


def spiked(entries, stream_key, source, target, blocks, factor):
    def block_of(dim):
        return (jnp.arange(entries.shape[dim]) // (entries.shape[dim] // blocks)).reshape((-1,) + (1,) * (entries.ndim - 1 - dim))

    near = jax.random.permutation(stream_key, blocks)[block_of(target)]
    far = (block_of(target) + blocks // 2) % blocks
    return jnp.where((block_of(source) == near) | (block_of(source) == far), factor * entries, entries)


def shard_levels(own_key, dims, pieces, low, high):
    factor_of, own = 1.0, jax.random.fold_in(own_key, 6)
    for dim, blocks in pieces:
        draws = jnp.exp(jax.random.uniform(jax.random.fold_in(own, dim), (blocks,), jnp.float32, low / len(pieces), high / len(pieces)))
        factor_of = factor_of * jnp.repeat(draws, dims[dim] // blocks).reshape([-1 if axis == dim else 1 for axis in range(len(dims))])
    return factor_of


def scatter_about(own_key, dims, deviation, limit, pieces=(), kind=jnp.bfloat16):
    level = shard_levels(own_key, dims, pieces, -0.22, 0.18) if pieces else 1.0
    values = jax.random.normal(own_key, dims, jnp.float32) * deviation * level
    return jnp.minimum(jnp.maximum(values, -limit), limit).astype(kind)


def gaussian_with(key, extent, scale, reach, cuts, heavy, kind=jnp.bfloat16):
    drawn = scale * jax.random.normal(key, extent, jnp.float32)
    if cuts:
        drawn = drawn * shard_levels(key, extent, cuts, -0.22, 0.18)
    return jnp.clip(spiked(drawn, jax.random.fold_in(key, 3), *heavy), -reach, reach).astype(kind)


def setup_inputs(seed: int = 0) -> dict:
    arg_keys = jax.random.split(jax.random.key(seed), 9)
    hidden_in = gaussian_with(arg_keys[0], (FRAMES, D), 1.0, 24.0, ((0, 256),), (0, 1, 256, 6.0))
    segment_ids = draw_segment_ids(jax.random.fold_in(arg_keys[8], 71), 0)
    frame_mask = draw_frame_mask(jax.random.fold_in(arg_keys[8], 71), 0)
    dw_kernel = scatter_about(arg_keys[3], (KERNEL, D), KERNEL ** -0.5, 1.0, ((1, 256),), jnp.float32)
    norm_scale = jnp.clip(1.0 + 0.18 * jax.random.normal(arg_keys[4], (D,), jnp.float32), 0.1, 1.9)
    norm_shift = scatter_about(arg_keys[5], (D,), 0.5, 3.0, ((0, 256),), jnp.float32)
    out_weight = scatter_about(arg_keys[6], (D, D), D ** -0.5, 0.15625, ((0, 256),))
    cotangent = scatter_about(arg_keys[7], (FRAMES, D), 1.0, 6.0, ((0, 256),))
    return {"hidden_in": hidden_in, "segment_ids": segment_ids, "frame_mask": frame_mask, "dw_kernel": dw_kernel, "norm_scale": norm_scale, "norm_shift": norm_shift, "out_weight": out_weight, "cotangent": cotangent}


def reference(hidden_in, segment_ids, frame_mask, dw_kernel, norm_scale, norm_shift, out_weight, cotangent):
    frames = hidden_in.shape[0]
    half = KERNEL // 2
    weight_col = frame_mask.astype(jnp.float32)[:, None]
    masked = jnp.where(frame_mask[:, None] == 1, hidden_in, jnp.zeros_like(hidden_in))
    padded_in = jnp.pad(masked.astype(jnp.float32), ((half, half), (0, 0)))
    seg_pad = jnp.pad(segment_ids, (half, half), constant_values=-1)
    conv = jnp.zeros((frames, hidden_in.shape[1]), jnp.float32)
    for offset in range(KERNEL):
        same_seg = (seg_pad[offset:offset + frames] == segment_ids)[:, None]
        conv = conv + jnp.where(same_seg, dw_kernel[offset] * padded_in[offset:offset + frames], 0.0)
    count = jnp.sum(weight_col)
    mean = lax.optimization_barrier(jnp.sum(weight_col * conv, axis=0)) / count
    centred = conv - mean
    variance = lax.optimization_barrier(jnp.sum(weight_col * centred * centred, axis=0)) / count
    inv_std = lax.rsqrt(variance + 1e-05)
    normed = centred * inv_std
    pre = norm_scale * normed + norm_shift
    sig = jax.nn.sigmoid(pre)
    act = (weight_col * pre * sig).astype(jnp.bfloat16)
    module_out = jnp.dot(act, out_weight, preferred_element_type=jnp.float32).astype(jnp.bfloat16)
    grad_act = jnp.dot(cotangent, out_weight.T, preferred_element_type=jnp.float32)
    grad_pre = weight_col * grad_act * sig * (1.0 + pre * (1.0 - sig))
    grad_scale = lax.optimization_barrier(jnp.sum(grad_pre * normed, axis=0))
    grad_shift = lax.optimization_barrier(jnp.sum(grad_pre, axis=0))
    grad_conv = weight_col * norm_scale * inv_std * (grad_pre - grad_shift / count - normed * grad_scale / count)
    grad_pad = jnp.pad(grad_conv, ((half, half), (0, 0)))
    grad_hidden = jnp.zeros_like(grad_conv)
    tap_rows = []
    for offset in range(KERNEL):
        same_fwd = (seg_pad[offset:offset + frames] == segment_ids)[:, None]
        tap_rows.append(lax.optimization_barrier(jnp.sum(jnp.where(same_fwd, grad_conv * padded_in[offset:offset + frames], 0.0), axis=0)))
        back = 2 * half - offset
        same_back = (seg_pad[back:back + frames] == segment_ids)[:, None]
        grad_hidden = grad_hidden + jnp.where(same_back, dw_kernel[offset] * grad_pad[back:back + frames], 0.0)
    grad_kernel = jnp.stack(tap_rows, axis=0)
    grad_hidden = (weight_col * grad_hidden).astype(jnp.bfloat16)
    grad_weight = jnp.dot(act.T, cotangent, preferred_element_type=jnp.float32)
    return (module_out, grad_hidden, grad_kernel, grad_scale, grad_shift, grad_weight)
```

```python
import jax
import jax.numpy as jnp
from jax import lax
from jax.experimental import pallas as pl
from jax.experimental.pallas import tpu as pltpu
from jax.sharding import Mesh, PartitionSpec as P

Z, X, Y, CORES = 8, 4, 4, 2
GROUP = Z * CORES
SETS = X * Y
KERNEL = 31
HALF = KERNEL // 2
D = 1536
ROWS = 128
OWN = D // (GROUP * SETS)
CHAN = OWN * SETS
HALO = 16
LANES = 128
BLOCK = CORES * ROWS
SPAN = BLOCK + 2 * HALO
SENT = ROWS + HALO
CHUNK = 64
MASK_LANE, HIGH_LANE, LOW_LANE, KEEP_LANE = CHAN, CHAN + 1, CHAN + 2, CHAN + 3
ALL = ("z", "x", "y", "core")
IN_GROUP = ("z", "core")
OVER_SETS = ("x", "y")
F32, BF16 = jnp.float32, jnp.bfloat16


def call(body, outs, ins, scratch, name, **more):
    return pl.pallas_call(
        body,
        out_shape=outs,
        scratch_shapes=scratch,
        name=name,
        compiler_params=pltpu.CompilerParams(vmem_limit_bytes=24 * 2**20),
        **more,
    )(*ins)


def vmem():
    return pl.BlockSpec(memory_space=pltpu.VMEM)


def smem():
    return pl.BlockSpec(memory_space=pltpu.SMEM)


def one_hot():
    col = lax.broadcasted_iota(jnp.int32, (1, 4 * LANES), 1)
    lane = col % LANES
    piece = col // LANES
    source = (
        (piece // 2) * (D // Z) + (lane // OWN) * (CORES * OWN) + (piece % 2) * OWN + lane % OWN
    )
    source = jnp.where(lane < CHAN, source, -1)
    row = lax.broadcasted_iota(jnp.int32, (2 * D // Z, 4 * LANES), 0)
    return jnp.where(row == source, 1.0, 0.0).astype(BF16)


def split_body(core_ref, own_ref, halo_ref, ext_ref, out_ref, rows_ref):
    @pl.when(core_ref[0] == 0)
    def _():
        rows_ref[0:HALO] = halo_ref[...]
        rows_ref[HALO:SENT] = own_ref[...]

    @pl.when(core_ref[0] != 0)
    def _():
        rows_ref[0:ROWS] = own_ref[...]
        rows_ref[ROWS:SENT] = halo_ref[...]

    ext = ext_ref[...].astype(F32)
    keep = ext[:, KEEP_LANE : KEEP_LANE + 1] > 0.5
    permute = one_hot()
    width = 2 * D // Z
    for part in range(Z // 2):
        piece = rows_ref[:, part * width : (part + 1) * width].astype(F32)
        piece = jnp.where(keep, piece, 0.0).astype(BF16)
        moved = jnp.dot(piece, permute, preferred_element_type=F32)
        for i in range(4):
            out_ref[4 * part + i] = (moved[:, i * LANES : (i + 1) * LANES] + ext).astype(BF16)


def segment_rows(x):
    seg = x[:, HIGH_LANE : HIGH_LANE + 1] * 256.0 + x[:, LOW_LANE : LOW_LANE + 1]
    return jnp.broadcast_to(seg, x.shape)


def mask_rows(x):
    return jnp.broadcast_to(x[:, MASK_LANE : MASK_LANE + 1], x.shape)


def conv_body(x_ref, wp_ref, conv_ref, stat_ref, par_ref, w_ref, wide_ref, xf_ref, seg_ref, m_ref, tmp_ref, wf_ref):
    tmp_ref[...] = jnp.zeros_like(tmp_ref)
    wf_ref[...] = jnp.zeros_like(wf_ref)
    for d in range(SETS):
        piece = wp_ref[d].astype(F32)
        high, mid, low = (piece[:, D + i * LANES : D + (i + 1) * LANES] for i in range(3))
        tmp_ref[d * OWN : (d + 1) * OWN] = high + mid + low
        wf_ref[d * OWN : (d + 1) * OWN] = piece[:, :D]
    wide = wf_ref[...].astype(BF16)
    wide_ref[...] = wide
    w_ref[...] = wide[:CHAN]
    par_ref[...] = tmp_ref[...].T[: par_ref.shape[0]]

    def block(b, carry):
        x = x_ref[b].astype(F32)
        xf_ref[...] = x
        seg_ref[...] = segment_rows(x)
        m_ref[b] = mask_rows(x[HALO : HALO + BLOCK])
        for chunk in range(BLOCK // CHUNK):
            base = HALO + chunk * CHUNK
            here = seg_ref[base : base + CHUNK]
            total = jnp.zeros((CHUNK, LANES), F32)
            for k in range(KERNEL):
                at = base + k - HALF
                near = jnp.where(seg_ref[at : at + CHUNK] == here, xf_ref[at : at + CHUNK], 0.0)
                total = total + par_ref[k : k + 1] * near
            conv_ref[b, chunk * CHUNK : (chunk + 1) * CHUNK] = total
        return carry

    lax.fori_loop(0, Z, block, 0)

    def first(b, carry):
        count, total = carry
        m = m_ref[b]
        return (
            count + jnp.sum(m.reshape(-1, 8, LANES), axis=0),
            total + jnp.sum((m * conv_ref[b]).reshape(-1, 8, LANES), axis=0),
        )

    zero = jnp.zeros((8, LANES), F32)
    count, total = lax.fori_loop(0, Z, first, (zero, zero))
    count = jnp.sum(count, axis=0, keepdims=True)
    total = jnp.sum(total, axis=0, keepdims=True)
    mean = total / count

    def second(b, spread):
        off = conv_ref[b] - mean
        return spread + jnp.sum((m_ref[b] * off * off).reshape(-1, 8, LANES), axis=0)

    spread = jnp.sum(lax.fori_loop(0, Z, second, zero), axis=0, keepdims=True)
    pad = jnp.zeros((5, LANES), F32)
    rows = jnp.concatenate([count, total, spread, pad], axis=0)
    for d in range(SETS):
        stat_ref[d] = rows


def moments(stat_ref):
    each = [stat_ref[d] for d in range(SETS)]
    count = sum(e[0:1] for e in each)
    mean = sum(e[1:2] for e in each) / count
    spread = sum(e[2:3] for e in each)
    for e in each:
        off = e[1:2] / e[0:1] - mean
        spread = spread + e[0:1] * off * off
    inv_std = lax.rsqrt(spread / count + 1e-05)
    return count, mean, inv_std


def grad_body(
    conv_ref, x_ref, cot_ref, wide_ref, par_ref, stat_ref,
    act_ref, gp_ref, nm_ref, first_ref, last_ref, sum_ref, gw_ref,
    total_ref, acc_ref,
):
    step = pl.program_id(0)
    count, mean, inv_std = moments(stat_ref)
    m = mask_rows(x_ref[0, HALO : HALO + BLOCK].astype(F32))
    scale = par_ref[KERNEL : KERNEL + 1]
    shift = par_ref[KERNEL + 1 : KERNEL + 2]
    normed = (conv_ref[0] - mean) * inv_std
    pre = scale * normed + shift
    sig = jax.nn.sigmoid(pre)
    act = (m * pre * sig).astype(BF16)
    act_ref[0] = act[:ROWS]
    act_ref[1] = act[ROWS:]
    cot = cot_ref[...].reshape(BLOCK, D)
    grad_act = lax.dot_general(
        cot, wide_ref[...], (((1,), (1,)), ((), ())), preferred_element_type=F32
    )
    gp = m * grad_act * sig * (1.0 + pre * (1.0 - sig))
    nm = m * normed
    gp_ref[0] = gp
    nm_ref[0] = nm
    lane = lax.broadcasted_iota(jnp.int32, (HALO, LANES), 1)
    for ref, at in ((first_ref, 0), (last_ref, BLOCK - HALO)):
        ref[0, 0] = gp[at : at + HALO].astype(BF16)
        ref[0, 1] = jnp.where(
            lane == MASK_LANE, m[at : at + HALO], nm[at : at + HALO]
        ).astype(BF16)

    @pl.when(step == 0)
    def _():
        total_ref[...] = jnp.zeros_like(total_ref)
        acc_ref[...] = jnp.zeros_like(acc_ref)

    acc_ref[0] += jnp.sum((gp * normed).reshape(-1, 8, LANES), axis=0)
    acc_ref[1] += jnp.sum(gp.reshape(-1, 8, LANES), axis=0)
    total_ref[...] += lax.dot_general(
        act, cot, (((0,), (0,)), ((), ())), preferred_element_type=F32
    )

    @pl.when(step == Z - 1)
    def _():
        rows = jnp.concatenate(
            [
                jnp.sum(acc_ref[0], axis=0, keepdims=True),
                jnp.sum(acc_ref[1], axis=0, keepdims=True),
                jnp.zeros((6, LANES), F32),
            ],
            axis=0,
        )
        for d in range(SETS):
            sum_ref[d] = rows
            gw_ref[d] = total_ref[d * OWN : (d + 1) * OWN].astype(BF16)


def back_body(
    set_ref, gp_ref, nm_ref, x_ref, par_ref, stat_ref, sum_ref, left_ref, right_ref, act_ref, gw_ref,
    pack_ref, gwp_ref, sums_ref,
    gc_ref, xf_ref, seg_ref, tap_ref, tmp_ref,
):
    count, mean, inv_std = moments(stat_ref)
    both = sum_ref[0]
    for d in range(1, SETS):
        both = both + sum_ref[d]
    sums_ref[...] = both
    gain = par_ref[KERNEL : KERNEL + 1] * inv_std
    by_norm = both[0:1] / count
    by_one = both[1:2] / count
    tap_ref[...] = jnp.zeros_like(tap_ref)
    where_am_i = set_ref[0]

    def outside(ref, b):
        gp = ref[b, 0].astype(F32)
        nm = ref[b, 1].astype(F32)
        return gain * (gp - by_one * mask_rows(nm) - by_norm * nm)

    def block(b, carry):
        x = x_ref[b].astype(F32)
        xf_ref[...] = x
        seg_ref[...] = segment_rows(x)
        before = jnp.where(where_am_i == 0, jnp.maximum(b - 1, 0), b)
        after = jnp.where(where_am_i == SETS - 1, jnp.minimum(b + 1, Z - 1), b)
        gc_ref[0:HALO] = outside(left_ref, before)
        gc_ref[HALO + BLOCK : SPAN] = outside(right_ref, after)
        m = mask_rows(x[HALO : HALO + BLOCK])
        gc_ref[HALO : HALO + BLOCK] = gain * (gp_ref[b] - by_one * m - by_norm * nm_ref[b])
        pieces = []
        for chunk in range(BLOCK // CHUNK):
            base = HALO + chunk * CHUNK
            here = seg_ref[base : base + CHUNK]
            centre = xf_ref[base : base + CHUNK]
            total = jnp.zeros((CHUNK, LANES), F32)
            for k in range(KERNEL):
                at = base + HALF - k
                near = jnp.where(seg_ref[at : at + CHUNK] == here, gc_ref[at : at + CHUNK], 0.0)
                total = total + par_ref[k : k + 1] * near
                tap_ref[k] += jnp.sum((centre * near).reshape(-1, 8, LANES), axis=0)
            pieces.append(total)
        for core in range(CORES):
            half = jnp.concatenate(
                pieces[core * (ROWS // CHUNK) : (core + 1) * (ROWS // CHUNK)], axis=0
            )
            half = half * m[core * ROWS : (core + 1) * ROWS]
            turned = pltpu.roll(half, CHAN, 1)
            at = CORES * b + core
            lane = lax.broadcasted_iota(jnp.int32, (ROWS, LANES), 1)
            pack_ref[at, 0:ROWS] = jnp.where(
                lane < CHAN, act_ref[at].astype(F32), turned
            ).astype(BF16)
            lane = lane[: ROWS // 2]
            pack_ref[at, ROWS : ROWS + ROWS // 2] = jnp.where(
                lane < LANES // 2, turned[: ROWS // 2], pltpu.roll(turned[ROWS // 2 :], LANES // 2, 1)
            ).astype(BF16)
        return carry

    lax.fori_loop(0, Z, block, 0)
    tmp_ref[...] = jnp.zeros_like(tmp_ref)
    tmp_ref[0:32] = jnp.sum(tap_ref[...], axis=1)
    tmp_ref[...] = tmp_ref[...].T
    for d in range(SETS):
        gwp_ref[d, :, :D] = gw_ref[d]
        taps = tmp_ref[d * OWN : (d + 1) * OWN]
        high = taps.astype(BF16)
        gwp_ref[d, :, D : D + LANES] = high
        gwp_ref[d, :, D + LANES : D + 2 * LANES] = (taps - high.astype(F32)).astype(BF16)


def join_body(pack_ref, w_ref, out_ref, gh_ref, four_ref):
    permute = one_hot()
    lane = lax.broadcasted_iota(jnp.int32, (ROWS // 2, LANES), 1)
    width = 2 * D // Z
    total = jnp.zeros((ROWS, D), F32)
    for part in range(Z // 2):
        for i in range(4):
            at = 4 * part + i
            main = pack_ref[at, 0:ROWS]
            total = total + jnp.dot(
                main[:, :CHAN], w_ref[at * CHAN : (at + 1) * CHAN], preferred_element_type=F32
            )
            main = main.astype(F32)
            rest = pack_ref[at, ROWS : ROWS + ROWS // 2].astype(F32)
            upper = jnp.where(lane < LANES // 2, rest, main[: ROWS // 2])
            lower = jnp.where(lane < LANES // 2, pltpu.roll(rest, LANES // 2, 1), main[ROWS // 2 :])
            turned = jnp.concatenate([upper, lower], axis=0)
            four_ref[:, i * LANES : (i + 1) * LANES] = pltpu.roll(turned, LANES - CHAN, 1).astype(BF16)
        gh_ref[:, part * width : (part + 1) * width] = lax.dot_general(
            four_ref[...], permute, (((1,), (1,)), ((), ())), preferred_element_type=F32
        ).astype(BF16)
    out_ref[...] = total.astype(BF16)


def shape(dims, kind):
    return jax.ShapeDtypeStruct(dims, kind)


def local(hidden_in, segment_ids, frame_mask, dw_kernel, norm_scale, norm_shift, out_weight, cotangent):
    core = lax.axis_index("core")
    here = lax.axis_index(ALL)
    this_set = lax.axis_index(OVER_SETS)

    with jax.named_scope("cotangent_of_group"):
        cot_all = lax.all_gather(cotangent, IN_GROUP)

    with jax.named_scope("rows_and_params"):
        params = jnp.concatenate([dw_kernel, norm_scale[None], norm_shift[None]], axis=0).T
        params = jnp.pad(params, ((0, 0), (0, LANES - params.shape[1])))
        high = lax.reduce_precision(params, 8, 7)
        rest = params - high
        mid = lax.reduce_precision(rest, 8, 7)
        low = rest - mid
        sent = jnp.concatenate([out_weight] + [p.astype(BF16) for p in (high, mid, low)], axis=1)
        sent = lax.optimization_barrier(jnp.broadcast_to(sent[None], (SETS,) + sent.shape))
        wp = lax.all_to_all(sent, OVER_SETS, 0, 0)

    with jax.named_scope("edge_frames"):
        edge = jnp.where(core == 1, hidden_in[ROWS - HALO :], hidden_in[:HALO])
        edge_mask = jnp.where(core == 1, frame_mask[ROWS - HALO :], frame_mask[:HALO])
        edge = jnp.where(edge_mask[:, None] == 1, edge, jnp.zeros_like(edge))
        last = Z * SETS * CORES - 1
        pairs = [(i, i + 1) for i in range(1, last, 2)] + [(i + 1, i) for i in range(1, last, 2)]
        halo = lax.ppermute(edge, ALL, pairs)

    with jax.named_scope("frames_to_channels"):
        mask = frame_mask.astype(F32)
        zeros, ones = jnp.zeros((HALO,), F32), jnp.ones((HALO,), F32)
        mask_col = jnp.where(
            core == 1, jnp.concatenate([mask, zeros]), jnp.concatenate([zeros, mask])
        )
        keep_col = jnp.where(core == 1, jnp.concatenate([mask, ones]), jnp.concatenate([ones, mask]))
        seg_pad = jnp.pad(segment_ids, (HALO, HALO), constant_values=-1)
        seg = lax.dynamic_slice_in_dim(seg_pad, here * ROWS + core * HALO, SENT)
        columns = (
            (MASK_LANE, mask_col),
            (HIGH_LANE, (seg >> 8).astype(F32)),
            (LOW_LANE, (seg & 255).astype(F32)),
            (KEEP_LANE, keep_col),
        )
        lane = lax.broadcasted_iota(jnp.int32, (SENT, LANES), 1)
        ext = jnp.zeros((SENT, LANES), F32)
        for at, column in columns:
            ext = jnp.where(lane == at, column[:, None], ext)
        frames = call(
            split_body,
            shape((GROUP, SENT, LANES), BF16),
            (core.reshape(1), hidden_in, halo, ext.astype(BF16)),
            [pltpu.VMEM((SENT, D), BF16)],
            "split",
            in_specs=[smem(), vmem(), vmem(), vmem()],
            out_specs=vmem(),
        )
        x = lax.all_to_all(frames, IN_GROUP, 0, 0).reshape(Z, SPAN, LANES)

    with jax.named_scope("conv"):
        conv, stat, par, rows, wide = call(
            conv_body,
            (
                shape((Z, BLOCK, LANES), F32),
                shape((SETS, 8, LANES), F32),
                shape((40, LANES), F32),
                shape((CHAN, D), BF16),
                shape((LANES, D), BF16),
            ),
            (x, wp),
            [
                pltpu.VMEM((SPAN, LANES), F32),
                pltpu.VMEM((SPAN, LANES), F32),
                pltpu.VMEM((Z, BLOCK, LANES), F32),
                pltpu.VMEM((LANES, LANES), F32),
                pltpu.VMEM((LANES, D), F32),
            ],
            "conv",
            in_specs=[vmem()] * 2,
            out_specs=[vmem()] * 5,
        )

    with jax.named_scope("weights_of_group"):
        w_all = lax.all_gather(rows, IN_GROUP, tiled=True)

    with jax.named_scope("norm_sums"):
        stat = lax.all_to_all(stat, OVER_SETS, 0, 0)

    with jax.named_scope("activation_grad"):
        whole = lambda *dims: pl.BlockSpec(dims, lambda i: (0,) * len(dims))
        act, gp, nm, first, last_rows, sums, gw = call(
            grad_body,
            (
                shape((GROUP, ROWS, LANES), BF16),
                shape((Z, BLOCK, LANES), F32),
                shape((Z, BLOCK, LANES), F32),
                shape((Z, 2, HALO, LANES), BF16),
                shape((Z, 2, HALO, LANES), BF16),
                shape((SETS, 8, LANES), F32),
                shape((SETS, OWN, D), BF16),
            ),
            (conv, x, cot_all, wide, par, stat),
            [pltpu.VMEM((LANES, D), F32), pltpu.VMEM((2, 8, LANES), F32)],
            "activation",
            grid=(Z,),
            in_specs=[
                pl.BlockSpec((1, BLOCK, LANES), lambda i: (i, 0, 0)),
                pl.BlockSpec((1, SPAN, LANES), lambda i: (i, 0, 0)),
                pl.BlockSpec((CORES, ROWS, D), lambda i: (i, 0, 0)),
                whole(LANES, D),
                whole(40, LANES),
                whole(SETS, 8, LANES),
            ],
            out_specs=[
                pl.BlockSpec((CORES, ROWS, LANES), lambda i: (i, 0, 0)),
                pl.BlockSpec((1, BLOCK, LANES), lambda i: (i, 0, 0)),
                pl.BlockSpec((1, BLOCK, LANES), lambda i: (i, 0, 0)),
                pl.BlockSpec((1, 2, HALO, LANES), lambda i: (i, 0, 0, 0)),
                pl.BlockSpec((1, 2, HALO, LANES), lambda i: (i, 0, 0, 0)),
                whole(SETS, 8, LANES),
                whole(SETS, OWN, D),
            ],
        )

    with jax.named_scope("edge_grads"):
        up = [(i, (i + 1) % SETS) for i in range(SETS)]
        down = [((i + 1) % SETS, i) for i in range(SETS)]
        left = lax.ppermute(last_rows, OVER_SETS, up)
        right = lax.ppermute(first, OVER_SETS, down)

    with jax.named_scope("norm_grad_sums"):
        sums = lax.all_to_all(sums, OVER_SETS, 0, 0)

    with jax.named_scope("conv_grad"):
        pack, gwp, both = call(
            back_body,
            (
                shape((GROUP, ROWS + ROWS // 2, LANES), BF16),
                shape((SETS, OWN, D + 2 * LANES), BF16),
                shape((8, LANES), F32),
            ),
            (this_set.reshape(1), gp, nm, x, par, stat, sums, left, right, act, gw),
            [
                pltpu.VMEM((SPAN, LANES), F32),
                pltpu.VMEM((SPAN, LANES), F32),
                pltpu.VMEM((SPAN, LANES), F32),
                pltpu.VMEM((32, 8, LANES), F32),
                pltpu.VMEM((LANES, LANES), F32),
            ],
            "conv_grad",
            in_specs=[smem()] + [vmem()] * 10,
            out_specs=[vmem()] * 3,
        )

    with jax.named_scope("weight_grad_sums"):
        gathered = lax.all_to_all(gwp, OVER_SETS, 0, 0)
        own = jnp.sum(gathered.astype(F32), axis=0)
        grad_weight = own[:, :D]
        grad_kernel = (own[:, D : D + KERNEL] + own[:, D + LANES : D + LANES + KERNEL]).T
        grad_scale = lax.dynamic_slice(both, (0, this_set * OWN), (1, OWN))[0]
        grad_shift = lax.dynamic_slice(both, (1, this_set * OWN), (1, OWN))[0]

    with jax.named_scope("channels_to_frames"):
        back = lax.all_to_all(pack, IN_GROUP, 0, 0)
        module_out, grad_hidden = call(
            join_body,
            (shape((ROWS, D), BF16), shape((ROWS, D), BF16)),
            (back, w_all),
            [pltpu.VMEM((ROWS, 4 * LANES), BF16)],
            "join",
            in_specs=[vmem()] * 2,
            out_specs=[vmem()] * 2,
        )
    return (module_out, grad_hidden, grad_kernel, grad_scale, grad_shift, grad_weight)


def solution(mesh):
    grid = Mesh(mesh.devices.reshape(Z, X, Y, CORES), ALL)
    return jax.shard_map(
        local,
        mesh=grid,
        in_specs=(P(ALL, None), P(), P(ALL), P(None, ALL), P(ALL), P(ALL), P(ALL, None), P(ALL, None)),
        out_specs=(P(ALL, None), P(ALL, None), P(None, ALL), P(ALL), P(ALL), P(ALL, None)),
        check_vma=False,
    )
```

```python
import jax
import jax.numpy as jnp
from jax import lax
from jax.experimental import pallas as pl
from jax.experimental.pallas import tpu as pltpu
from jax.sharding import Mesh, PartitionSpec as P

Z, X, Y, CORES = 8, 4, 4, 2
GROUP = Z * CORES
SETS = X * Y
KERNEL = 31
HALF = KERNEL // 2
D = 1536
ROWS = 128
OWN = D // (GROUP * SETS)
CHAN = OWN * SETS
HALO = 16
LANES = 128
BLOCK = CORES * ROWS
SPAN = BLOCK + 2 * HALO
SENT = ROWS + HALO
CHUNK = 64
WIDE = D + LANES
PART = 40
MASK_LANE, PREV_LANE, NEXT_LANE = CHAN, CHAN + 1, CHAN + 2
ALL = ("z", "x", "y", "core")
IN_GROUP = ("z", "core")
OVER_SETS = ("x", "y")
F32, BF16 = jnp.float32, jnp.bfloat16


def call(body, outs, ins, scratch, name, work=0, **more):
    if work:
        more["cost_estimate"] = pl.CostEstimate(flops=work, bytes_accessed=2**20, transcendentals=0)
    return pl.pallas_call(
        body,
        out_shape=outs,
        scratch_shapes=scratch,
        name=name,
        compiler_params=pltpu.CompilerParams(vmem_limit_bytes=64 * 2**20),
        **more,
    )(*ins)


def vmem():
    return pl.BlockSpec(memory_space=pltpu.VMEM)


def hbm():
    return pl.BlockSpec(memory_space=pltpu.HBM)


def parts(x):
    high = x.astype(BF16).astype(F32)
    mid = (x - high).astype(BF16).astype(F32)
    return high, mid, (x - high - mid).astype(BF16).astype(F32)


def smem():
    return pl.BlockSpec(memory_space=pltpu.SMEM)


def one_hot():
    col = lax.broadcasted_iota(jnp.int32, (1, 4 * LANES), 1)
    lane = col % LANES
    piece = col // LANES
    source = (
        (piece // 2) * (D // Z) + (lane // OWN) * (CORES * OWN) + (piece % 2) * OWN + lane % OWN
    )
    source = jnp.where(lane < CHAN, source, -1)
    row = lax.broadcasted_iota(jnp.int32, (2 * D // Z, 4 * LANES), 0)
    return jnp.where(row == source, 1.0, 0.0).astype(BF16)


def prep_body(
    core_ref, seg_ref, taps_hbm, scale_hbm, shift_hbm, mask_hbm, w_hbm, own_hbm,
    wp_ref, ext_ref, own_ref, edge_ref,
    tmp_ref, taps_ref, scale_ref, shift_ref, mask_ref, w_ref, sem,
):
    pairs = (
        (taps_hbm, taps_ref), (scale_hbm, scale_ref), (shift_hbm, shift_ref),
        (mask_hbm, mask_ref), (w_hbm, w_ref), (own_hbm, own_ref),
    )
    copies = [pltpu.make_async_copy(a, b, sem.at[i]) for i, (a, b) in enumerate(pairs)]
    for copy in copies:
        copy.start()
    tmp_ref[...] = jnp.zeros_like(tmp_ref)
    for copy in copies:
        copy.wait()
    tmp_ref[KERNEL : KERNEL + 1, 0:OWN] = scale_ref[...]
    tmp_ref[KERNEL + 1 : KERNEL + 2, 0:OWN] = shift_ref[...]
    rows = tmp_ref[...].T
    tmp_ref[0:8] = rows[0:8]
    tmp_ref[0:OWN, 0:KERNEL] = taps_ref[...]
    high, mid, low = parts(tmp_ref[0:8])
    side = high + pltpu.roll(mid, PART, 1) + pltpu.roll(low, 2 * PART, 1)
    side = side[0:OWN].astype(BF16)
    for d in range(SETS):
        wp_ref[d, :, 0:D] = w_ref[...]
        wp_ref[d, :, D:WIDE] = side
    seg = seg_ref[...]
    own = seg[:, HALO : HALO + ROWS]
    before = jnp.zeros((1, ROWS), F32)
    after = jnp.zeros((1, ROWS), F32)
    for j in range(1, HALF + 1):
        before = before + jnp.where(seg[:, HALO - j : HALO - j + ROWS] == own, 1.0, 0.0)
        after = after + jnp.where(seg[:, HALO + j : HALO + j + ROWS] == own, 1.0, 0.0)
    tmp_ref[...] = jnp.zeros_like(tmp_ref)
    tmp_ref[MASK_LANE : MASK_LANE + 1] = mask_ref[...].astype(F32)
    tmp_ref[PREV_LANE : PREV_LANE + 1] = before
    tmp_ref[NEXT_LANE : NEXT_LANE + 1] = after
    ext = tmp_ref[...].T
    ext_ref[...] = ext
    keep = ext[:, MASK_LANE : MASK_LANE + 1] > 0.5
    own = jnp.where(keep, own_ref[...].astype(F32), 0.0).astype(BF16)
    own_ref[...] = own
    edge_ref[...] = jnp.where(core_ref[0] == 0, own[0:HALO].astype(F32), own[ROWS - HALO :].astype(F32)).astype(BF16)


def split_body(core_ref, own_ref, halo_ref, ext_ref, out_ref, rows_ref, side_ref):
    own = own_ref[...]
    none = jnp.zeros((HALO, LANES), F32)

    @pl.when(core_ref[0] == 0)
    def _():
        rows_ref[0:HALO] = halo_ref[...]
        rows_ref[HALO:SENT] = own
        side_ref[0:HALO] = none
        side_ref[HALO:SENT] = ext_ref[...]

    @pl.when(core_ref[0] != 0)
    def _():
        rows_ref[0:ROWS] = own
        rows_ref[ROWS:SENT] = halo_ref[...]
        side_ref[0:ROWS] = ext_ref[...]
        side_ref[ROWS:SENT] = none

    ext = side_ref[...]
    permute = one_hot()
    width = 2 * D // Z
    for part in range(Z // 2):
        piece = rows_ref[:, part * width : (part + 1) * width]
        moved = jnp.dot(piece, permute, preferred_element_type=F32)
        for i in range(4):
            out_ref[4 * part + i] = (moved[:, i * LANES : (i + 1) * LANES] + ext).astype(BF16)


def lane_rows(x, lane):
    return jnp.broadcast_to(x[:, lane : lane + 1], x.shape)


def mask_rows(x):
    return lane_rows(x, MASK_LANE)


def near_rows(ref, base, offset, before, after):
    rows = ref[base + offset : base + offset + CHUNK]
    if offset == 0:
        return rows
    same = before >= -offset if offset < 0 else after >= offset
    return jnp.where(same, rows, 0.0)


def conv_body(
    x_ref, wp_ref, conv_ref, stat_ref, par_ref, w_ref, wide_ref,
    xf_ref, prev_ref, next_ref, tmp_ref, wf_ref, run_ref,
):
    step = pl.program_id(0)

    @pl.when(step == 0)
    def _():
        wf_ref[CHAN:] = jnp.zeros((LANES - CHAN, WIDE), F32)
        for d in range(SETS):
            wf_ref[d * OWN : (d + 1) * OWN] = wp_ref[d].astype(F32)
        wide = wf_ref[:, 0:D].astype(BF16)
        wide_ref[...] = wide
        w_ref[...] = wide[:CHAN]
        tmp_ref[...] = wf_ref[:, D:WIDE].T
        par_ref[...] = tmp_ref[0:PART] + tmp_ref[PART : 2 * PART] + tmp_ref[2 * PART : 3 * PART]
        run_ref[...] = jnp.zeros_like(run_ref)

    x = x_ref[0].astype(F32)
    xf_ref[...] = x
    inside = x[HALO : HALO + BLOCK]
    prev_ref[...] = lane_rows(inside, PREV_LANE)
    next_ref[...] = lane_rows(inside, NEXT_LANE)
    for chunk in range(BLOCK // CHUNK):
        at = slice(chunk * CHUNK, (chunk + 1) * CHUNK)
        before, after = prev_ref[at], next_ref[at]
        total = jnp.zeros((CHUNK, LANES), F32)
        for k in range(KERNEL):
            near = near_rows(xf_ref, HALO + chunk * CHUNK, k - HALF, before, after)
            total = total + par_ref[k : k + 1] * near
        conv_ref[0, at] = total

    rows = lambda v: jnp.sum(jnp.sum(v.reshape(-1, 8, LANES), axis=0), axis=0, keepdims=True)
    m = mask_rows(inside)
    conv = conv_ref[0]
    here = rows(m)
    mean_here = rows(m * conv) / here
    off = conv - mean_here
    count, mean, spread = run_ref[0:1], run_ref[1:2], run_ref[2:3]
    both = count + here
    apart = mean_here - mean
    run_ref[0:1] = both
    run_ref[1:2] = mean + apart * (here / both)
    run_ref[2:3] = spread + rows(m * off * off) + apart * apart * (count * here / both)

    @pl.when(step == Z - 1)
    def _():
        for d in range(SETS):
            stat_ref[d] = run_ref[...]


def moments(stat_ref):
    each = [stat_ref[d] for d in range(SETS)]
    count = sum(e[0:1] for e in each)
    mean = sum(e[0:1] * e[1:2] for e in each) / count
    spread = sum(e[2:3] for e in each)
    for e in each:
        off = e[1:2] - mean
        spread = spread + e[0:1] * off * off
    inv_std = lax.rsqrt(spread / count + 1e-05)
    return count, mean, inv_std


def grad_body(
    conv_ref, x_ref, wide_ref, par_ref, stat_ref, cot_hbm,
    act_ref, gp_ref, nm_ref, first_ref, last_ref, gw_ref,
    total_ref, acc_ref, mom_ref, cot_ref, sem,
):
    step = pl.program_id(0)

    def fetch(i):
        rows = pl.ds(i * CORES, CORES)
        return pltpu.make_async_copy(cot_hbm.at[rows], cot_ref.at[rows], sem.at[i])

    @pl.when(step == 0)
    def _():
        for i in range(Z):
            fetch(i).start()

    @pl.when(step == 0)
    def _():
        total_ref[...] = jnp.zeros_like(total_ref)
        acc_ref[...] = jnp.zeros_like(acc_ref)
        count, mean, inv_std = moments(stat_ref)
        mom_ref[0:1] = mean
        mom_ref[1:2] = inv_std

    mean, inv_std = mom_ref[0:1], mom_ref[1:2]
    m = mask_rows(x_ref[0, HALO : HALO + BLOCK].astype(F32))
    scale = par_ref[KERNEL : KERNEL + 1]
    shift = par_ref[KERNEL + 1 : KERNEL + 2]
    normed = (conv_ref[0] - mean) * inv_std
    pre = scale * normed + shift
    sig = jax.nn.sigmoid(pre)
    act = (m * pre * sig).astype(BF16)
    act_ref[0] = act[:ROWS]
    act_ref[1] = act[ROWS:]
    fetch(step).wait()
    cot = cot_ref[pl.ds(step * CORES, CORES)].reshape(BLOCK, D)
    grad_act = lax.dot_general(
        cot, wide_ref[...], (((1,), (1,)), ((), ())), preferred_element_type=F32
    )
    gp = m * grad_act * sig * (1.0 + pre * (1.0 - sig))
    nm = m * normed
    gp_ref[0] = gp
    nm_ref[0] = nm
    lane = lax.broadcasted_iota(jnp.int32, (HALO, LANES), 1)
    for ref, at in ((first_ref, 0), (last_ref, BLOCK - HALO)):
        ref[0, 0] = gp[at : at + HALO].astype(BF16)
        ref[0, 1] = jnp.where(
            lane == MASK_LANE, m[at : at + HALO], nm[at : at + HALO]
        ).astype(BF16)

    acc_ref[0] += jnp.sum((gp * normed).reshape(-1, 8, LANES), axis=0)
    acc_ref[1] += jnp.sum(gp.reshape(-1, 8, LANES), axis=0)
    total_ref[...] += lax.dot_general(
        act, cot, (((0,), (0,)), ((), ())), preferred_element_type=F32
    )

    @pl.when(step == Z - 1)
    def _():
        sums = [jnp.sum(acc_ref[i], axis=0, keepdims=True) for i in range(2)]
        rows = jnp.concatenate(list(parts(sums[0])) + list(parts(sums[1])), axis=0).astype(BF16)
        for d in range(SETS):
            gw_ref[d, :, 0:D] = total_ref[d * OWN : (d + 1) * OWN].astype(BF16)
            gw_ref[d, :, D:WIDE] = rows


def back_body(
    set_ref, gp_ref, nm_ref, x_ref, act_ref, par_ref, stat_ref, sum_ref, left_ref, right_ref,
    pack_ref, taps_ref, sums_ref,
    gc_ref, xf_ref, prev_ref, next_ref, tap_ref, run_ref,
):
    b = pl.program_id(0)

    @pl.when(b == 0)
    def _():
        count, mean, inv_std = moments(stat_ref)
        each = sum_ref[0, :, D:WIDE].astype(F32)
        for d in range(1, SETS):
            each = each + sum_ref[d, :, D:WIDE].astype(F32)
        scale_sum = each[0:1] + each[1:2] + each[2:3]
        shift_sum = each[3:4] + each[4:5] + each[5:6]
        sums_ref[...] = jnp.concatenate([scale_sum, shift_sum, jnp.zeros((6, LANES), F32)], axis=0)
        run_ref[0:1] = par_ref[KERNEL : KERNEL + 1] * inv_std
        run_ref[1:2] = scale_sum / count
        run_ref[2:3] = shift_sum / count
        tap_ref[...] = jnp.zeros_like(tap_ref)

    gain, by_norm, by_one = run_ref[0:1], run_ref[1:2], run_ref[2:3]
    where_am_i = set_ref[0]

    def outside(ref, at):
        gp = ref[at, 0].astype(F32)
        nm = ref[at, 1].astype(F32)
        return gain * (gp - by_one * mask_rows(nm) - by_norm * nm)

    x = x_ref[0, HALO : HALO + BLOCK].astype(F32)
    xf_ref[...] = x
    prev_ref[...] = lane_rows(x, PREV_LANE)
    next_ref[...] = lane_rows(x, NEXT_LANE)
    gc_ref[0:HALO] = outside(left_ref, jnp.where(where_am_i == 0, jnp.maximum(b - 1, 0), b))
    gc_ref[HALO + BLOCK : SPAN] = outside(
        right_ref, jnp.where(where_am_i == SETS - 1, jnp.minimum(b + 1, Z - 1), b)
    )
    m = mask_rows(x)
    gc_ref[HALO : HALO + BLOCK] = gain * (gp_ref[0] - by_one * m - by_norm * nm_ref[0])
    pieces = []
    for chunk in range(BLOCK // CHUNK):
        at = slice(chunk * CHUNK, (chunk + 1) * CHUNK)
        before, after, centre = prev_ref[at], next_ref[at], xf_ref[at]
        total = jnp.zeros((CHUNK, LANES), F32)
        for k in range(KERNEL):
            near = near_rows(gc_ref, HALO + chunk * CHUNK, HALF - k, before, after)
            total = total + par_ref[k : k + 1] * near
            tap_ref[k] += jnp.sum((centre * near).reshape(-1, 8, LANES), axis=0)
        pieces.append(total)
    for core in range(CORES):
        half = jnp.concatenate(
            pieces[core * (ROWS // CHUNK) : (core + 1) * (ROWS // CHUNK)], axis=0
        )
        half = half * m[core * ROWS : (core + 1) * ROWS]
        turned = pltpu.roll(half, CHAN, 1)
        lane = lax.broadcasted_iota(jnp.int32, (ROWS, LANES), 1)
        pack_ref[core, 0:ROWS] = jnp.where(
            lane < CHAN, act_ref[core].astype(F32), turned
        ).astype(BF16)
        lane = lane[: ROWS // 2]
        pack_ref[core, ROWS : ROWS + ROWS // 2] = jnp.where(
            lane < LANES // 2, turned[: ROWS // 2], pltpu.roll(turned[ROWS // 2 :], LANES // 2, 1)
        ).astype(BF16)

    @pl.when(b == Z - 1)
    def _():
        taps_ref[...] = jnp.sum(tap_ref[...], axis=1)


def join_body(pack_ref, w_hbm, out_ref, gh_ref, four_ref, total_ref, w_ref, sem):
    step = pl.program_id(0)
    width = 4 * CHAN

    def fetch(i):
        rows = pl.ds(pl.multiple_of(i * width, width), width)
        return pltpu.make_async_copy(w_hbm.at[rows], w_ref.at[i], sem.at[i])

    @pl.when(step == 0)
    def _():
        for i in range(Z // 2):
            fetch(i).start()

    fetch(step).wait()
    lane = lax.broadcasted_iota(jnp.int32, (ROWS // 2, LANES), 1)

    @pl.when(step == 0)
    def _():
        total_ref[...] = jnp.zeros_like(total_ref)

    total = total_ref[...]
    for i in range(4):
        main = pack_ref[i, 0:ROWS]
        total = total + jnp.dot(
            main[:, :CHAN], w_ref[step, i * CHAN : (i + 1) * CHAN], preferred_element_type=F32
        )
        main = main.astype(F32)
        rest = pack_ref[i, ROWS : ROWS + ROWS // 2].astype(F32)
        upper = jnp.where(lane < LANES // 2, rest, main[: ROWS // 2])
        lower = jnp.where(lane < LANES // 2, pltpu.roll(rest, LANES // 2, 1), main[ROWS // 2 :])
        turned = jnp.concatenate([upper, lower], axis=0)
        four_ref[:, i * LANES : (i + 1) * LANES] = pltpu.roll(turned, LANES - CHAN, 1).astype(BF16)
    total_ref[...] = total
    gh_ref[...] = lax.dot_general(
        four_ref[...], one_hot(), (((1,), (1,)), ((), ())), preferred_element_type=F32
    ).astype(BF16)

    @pl.when(step == Z // 2 - 1)
    def _():
        out_ref[...] = total.astype(BF16)


def shape(dims, kind):
    return jax.ShapeDtypeStruct(dims, kind)


def local(hidden_in, segment_ids, frame_mask, dw_kernel, norm_scale, norm_shift, out_weight, cotangent):
    core = lax.axis_index("core")
    here = lax.axis_index(ALL)
    this_set = lax.axis_index(OVER_SETS)

    with jax.named_scope("cotangent_of_group"):
        cot_all = lax.all_gather(cotangent, IN_GROUP)

    with jax.named_scope("prepare"):
        seg = lax.dynamic_slice_in_dim(
            jnp.pad(segment_ids, (HALO, LANES - HALO), constant_values=-1), here * ROWS, 2 * LANES
        )
        row = lambda v: v.reshape(1, -1)
        wp, ext, own, edge = call(
            prep_body,
            (
                shape((SETS, OWN, WIDE), BF16),
                shape((ROWS, LANES), F32),
                shape((ROWS, D), BF16),
                shape((HALO, D), BF16),
            ),
            (core.reshape(1), row(seg), dw_kernel.T, row(norm_scale), row(norm_shift), row(frame_mask), out_weight, hidden_in),
            [
                pltpu.VMEM((LANES, LANES), F32),
                pltpu.VMEM((OWN, KERNEL), F32),
                pltpu.VMEM((1, OWN), F32),
                pltpu.VMEM((1, OWN), F32),
                pltpu.VMEM((1, ROWS), jnp.int32),
                pltpu.VMEM((OWN, D), BF16),
                pltpu.SemaphoreType.DMA((6,)),
            ],
            "prepare",
            in_specs=[smem(), vmem()] + [hbm()] * 6,
            out_specs=[vmem()] * 4,
        )

    with jax.named_scope("edge_frames"):
        last = Z * SETS * CORES - 1
        pairs = [(i, i + 1) for i in range(1, last, 2)] + [(i + 1, i) for i in range(1, last, 2)]
        halo = lax.ppermute(edge, ALL, pairs)

    with jax.named_scope("rows_and_params"):
        wp = lax.all_to_all(wp, OVER_SETS, 0, 0)

    with jax.named_scope("frames_to_channels"):
        frames = call(
            split_body,
            shape((GROUP, SENT, LANES), BF16),
            (core.reshape(1), own, halo, ext),
            [pltpu.VMEM((SENT, D), BF16), pltpu.VMEM((SENT, LANES), F32)],
            "split",
            in_specs=[smem(), vmem(), vmem(), vmem()],
            out_specs=vmem(),
        )
        frames, wp = lax.optimization_barrier((frames, wp))
        x = lax.all_to_all(frames, IN_GROUP, 0, 0).reshape(Z, SPAN, LANES)

    whole = lambda *dims: pl.BlockSpec(dims, lambda i: (0,) * len(dims))
    each = lambda *dims: pl.BlockSpec(dims, lambda i: (i,) + (0,) * (len(dims) - 1))

    with jax.named_scope("conv"):
        conv, stat, par, rows, wide = call(
            conv_body,
            (
                shape((Z, BLOCK, LANES), F32),
                shape((SETS, 8, LANES), F32),
                shape((PART, LANES), F32),
                shape((CHAN, D), BF16),
                shape((LANES, D), BF16),
            ),
            (x, wp),
            [
                pltpu.VMEM((SPAN, LANES), F32),
                pltpu.VMEM((BLOCK, LANES), F32),
                pltpu.VMEM((BLOCK, LANES), F32),
                pltpu.VMEM((LANES, LANES), F32),
                pltpu.VMEM((LANES, WIDE), F32),
                pltpu.VMEM((8, LANES), F32),
            ],
            "conv",
            work=6 * 10**9,
            grid=(Z,),
            in_specs=[each(1, SPAN, LANES), whole(SETS, OWN, WIDE)],
            out_specs=[
                each(1, BLOCK, LANES),
                whole(SETS, 8, LANES),
                whole(PART, LANES),
                whole(CHAN, D),
                whole(LANES, D),
            ],
        )

    with jax.named_scope("weights_of_group"):
        w_all = lax.all_gather(rows, IN_GROUP, tiled=True)

    with jax.named_scope("norm_sums"):
        stat = lax.all_to_all(stat, OVER_SETS, 0, 0)

    with jax.named_scope("activation_grad"):
        act, gp, nm, first, last_rows, gw = call(
            grad_body,
            (
                shape((GROUP, ROWS, LANES), BF16),
                shape((Z, BLOCK, LANES), F32),
                shape((Z, BLOCK, LANES), F32),
                shape((Z, 2, HALO, LANES), BF16),
                shape((Z, 2, HALO, LANES), BF16),
                shape((SETS, OWN, WIDE), BF16),
            ),
            (conv, x, wide, par, stat, cot_all),
            [
                pltpu.VMEM((LANES, D), F32),
                pltpu.VMEM((2, 8, LANES), F32),
                pltpu.VMEM((8, LANES), F32),
                pltpu.VMEM((GROUP, ROWS, D), BF16),
                pltpu.SemaphoreType.DMA((Z,)),
            ],
            "activation",
            grid=(Z,),
            in_specs=[
                pl.BlockSpec((1, BLOCK, LANES), lambda i: (i, 0, 0)),
                pl.BlockSpec((1, SPAN, LANES), lambda i: (i, 0, 0)),
                whole(LANES, D),
                whole(PART, LANES),
                whole(SETS, 8, LANES),
                hbm(),
            ],
            out_specs=[
                pl.BlockSpec((CORES, ROWS, LANES), lambda i: (i, 0, 0)),
                pl.BlockSpec((1, BLOCK, LANES), lambda i: (i, 0, 0)),
                pl.BlockSpec((1, BLOCK, LANES), lambda i: (i, 0, 0)),
                pl.BlockSpec((1, 2, HALO, LANES), lambda i: (i, 0, 0, 0)),
                pl.BlockSpec((1, 2, HALO, LANES), lambda i: (i, 0, 0, 0)),
                whole(SETS, OWN, WIDE),
            ],
        )

    with jax.named_scope("edge_grads"):
        up = [(i, (i + 1) % SETS) for i in range(SETS)]
        down = [((i + 1) % SETS, i) for i in range(SETS)]
        left = lax.ppermute(last_rows, OVER_SETS, up)
        right = lax.ppermute(first, OVER_SETS, down)

    with jax.named_scope("norm_grad_sums"):
        gw = lax.all_to_all(gw, OVER_SETS, 0, 0)

    with jax.named_scope("conv_grad"):
        pack, taps, both = call(
            back_body,
            (
                shape((GROUP, ROWS + ROWS // 2, LANES), BF16),
                shape((32, LANES), F32),
                shape((8, LANES), F32),
            ),
            (this_set.reshape(1), gp, nm, x, act, par, stat, gw, left, right),
            [
                pltpu.VMEM((SPAN, LANES), F32),
                pltpu.VMEM((BLOCK, LANES), F32),
                pltpu.VMEM((BLOCK, LANES), F32),
                pltpu.VMEM((BLOCK, LANES), F32),
                pltpu.VMEM((32, 8, LANES), F32),
                pltpu.VMEM((8, LANES), F32),
            ],
            "conv_grad",
            work=10**10,
            grid=(Z,),
            in_specs=[
                smem(),
                each(1, BLOCK, LANES),
                each(1, BLOCK, LANES),
                each(1, SPAN, LANES),
                each(CORES, ROWS, LANES),
                whole(PART, LANES),
                whole(SETS, 8, LANES),
                whole(SETS, OWN, WIDE),
                whole(Z, 2, HALO, LANES),
                whole(Z, 2, HALO, LANES),
            ],
            out_specs=[each(CORES, ROWS + ROWS // 2, LANES), whole(32, LANES), whole(8, LANES)],
        )

    with jax.named_scope("channels_to_frames"):
        back = lax.all_to_all(pack, IN_GROUP, 0, 0)

    with jax.named_scope("sums_of_taps"):
        for axis, size in (("x", X), ("y", Y)):
            moved = [
                lax.ppermute(taps, axis, [(i, (i + by) % size) for i in range(size)])
                for by in range(1, size)
            ]
            taps = taps + sum(moved)
        at = this_set * OWN
        grad_kernel = lax.dynamic_slice(taps, (0, at), (KERNEL, OWN))
        grad_scale = lax.dynamic_slice(both, (0, at), (1, OWN))[0]
        grad_shift = lax.dynamic_slice(both, (1, at), (1, OWN))[0]

    with jax.named_scope("weight_grad_sums"):
        grad_weight = jnp.sum(gw[:, :, :D].astype(F32), axis=0)

    with jax.named_scope("join"):
        width = 2 * D // Z
        module_out, grad_hidden = call(
            join_body,
            (shape((ROWS, D), BF16), shape((ROWS, D), BF16)),
            (back, w_all),
            [
                pltpu.VMEM((ROWS, 4 * LANES), BF16),
                pltpu.VMEM((ROWS, D), F32),
                pltpu.VMEM((Z // 2, width, D), BF16),
                pltpu.SemaphoreType.DMA((Z // 2,)),
            ],
            "join",
            grid=(Z // 2,),
            in_specs=[
                pl.BlockSpec((4, ROWS + ROWS // 2, LANES), lambda i: (i, 0, 0)),
                hbm(),
            ],
            out_specs=[
                pl.BlockSpec((ROWS, D), lambda i: (0, 0)),
                pl.BlockSpec((ROWS, width), lambda i: (0, i)),
            ],
        )
    return (module_out, grad_hidden, grad_kernel, grad_scale, grad_shift, grad_weight)


def solution(mesh):
    grid = Mesh(mesh.devices.reshape(Z, X, Y, CORES), ALL)
    return jax.shard_map(
        local,
        mesh=grid,
        in_specs=(P(ALL, None), P(), P(ALL), P(None, ALL), P(ALL), P(ALL), P(ALL, None), P(ALL, None)),
        out_specs=(P(ALL, None), P(ALL, None), P(None, ALL), P(ALL), P(ALL), P(ALL, None)),
        check_vma=False,
    )
```

```python
import jax
import jax.numpy as jnp
from jax import lax
from jax.experimental import pallas as pl
from jax.experimental.pallas import tpu as pltpu
from jax.sharding import Mesh, PartitionSpec as P

Z, X, Y, CORES = 8, 4, 4, 2
GROUP = Z * CORES
SETS = X * Y
KERNEL = 31
HALF = KERNEL // 2
D = 1536
ROWS = 128
OWN = D // (GROUP * SETS)
CHAN = OWN * SETS
HALO = 16
LANES = 128
BLOCK = CORES * ROWS
SPAN = BLOCK + 2 * HALO
SENT = ROWS + HALO
CHUNK = 64
WIDE = D + LANES
PART = 40
MASK_LANE, PREV_LANE, NEXT_LANE = CHAN, CHAN + 1, CHAN + 2
ALL = ("z", "x", "y", "core")
IN_GROUP = ("z", "core")
OVER_SETS = ("x", "y")
F32, BF16 = jnp.float32, jnp.bfloat16


def call(body, outs, ins, scratch, name, limit=64, work=0, **more):
    if work:
        more["cost_estimate"] = pl.CostEstimate(flops=work, bytes_accessed=2**20, transcendentals=0)
    return pl.pallas_call(
        body,
        out_shape=outs,
        scratch_shapes=scratch,
        name=name,
        compiler_params=pltpu.CompilerParams(vmem_limit_bytes=limit * 2**20),
        **more,
    )(*ins)


def vmem():
    return pl.BlockSpec(memory_space=pltpu.VMEM)


def hbm():
    return pl.BlockSpec(memory_space=pltpu.HBM)


def parts(x):
    high = x.astype(BF16).astype(F32)
    mid = (x - high).astype(BF16).astype(F32)
    return high, mid, (x - high - mid).astype(BF16).astype(F32)


def smem():
    return pl.BlockSpec(memory_space=pltpu.SMEM)


def one_hot():
    col = lax.broadcasted_iota(jnp.int32, (1, 4 * LANES), 1)
    lane = col % LANES
    piece = col // LANES
    source = (
        (piece // 2) * (D // Z) + (lane // OWN) * (CORES * OWN) + (piece % 2) * OWN + lane % OWN
    )
    source = jnp.where(lane < CHAN, source, -1)
    row = lax.broadcasted_iota(jnp.int32, (2 * D // Z, 4 * LANES), 0)
    return jnp.where(row == source, 1.0, 0.0).astype(BF16)


def prep_body(
    core_ref, seg_ref, taps_hbm, scale_hbm, shift_hbm, mask_hbm, w_hbm, own_hbm,
    wp_ref, ext_ref, own_ref, edge_ref,
    tmp_ref, taps_ref, scale_ref, shift_ref, mask_ref, w_ref, sem,
):
    pairs = (
        (taps_hbm, taps_ref), (scale_hbm, scale_ref), (shift_hbm, shift_ref),
        (mask_hbm, mask_ref), (w_hbm, w_ref), (own_hbm, own_ref),
    )
    copies = [pltpu.make_async_copy(a, b, sem.at[i]) for i, (a, b) in enumerate(pairs)]
    for copy in copies:
        copy.start()
    tmp_ref[...] = jnp.zeros_like(tmp_ref)
    for copy in copies:
        copy.wait()
    tmp_ref[KERNEL : KERNEL + 1, 0:OWN] = scale_ref[...]
    tmp_ref[KERNEL + 1 : KERNEL + 2, 0:OWN] = shift_ref[...]
    rows = tmp_ref[...].T
    tmp_ref[0:8] = rows[0:8]
    tmp_ref[0:OWN, 0:KERNEL] = taps_ref[...]
    high, mid, low = parts(tmp_ref[0:8])
    side = high + pltpu.roll(mid, PART, 1) + pltpu.roll(low, 2 * PART, 1)
    side = side[0:OWN].astype(BF16)
    for d in range(SETS):
        wp_ref[d, :, 0:D] = w_ref[...]
        wp_ref[d, :, D:WIDE] = side
    seg = seg_ref[...]
    own = seg[:, HALO : HALO + ROWS]
    before = jnp.zeros((1, ROWS), F32)
    after = jnp.zeros((1, ROWS), F32)
    for j in range(1, HALF + 1):
        before = before + jnp.where(seg[:, HALO - j : HALO - j + ROWS] == own, 1.0, 0.0)
        after = after + jnp.where(seg[:, HALO + j : HALO + j + ROWS] == own, 1.0, 0.0)
    tmp_ref[...] = jnp.zeros_like(tmp_ref)
    tmp_ref[MASK_LANE : MASK_LANE + 1] = mask_ref[...].astype(F32)
    tmp_ref[PREV_LANE : PREV_LANE + 1] = before
    tmp_ref[NEXT_LANE : NEXT_LANE + 1] = after
    ext = tmp_ref[...].T
    ext_ref[...] = ext
    keep = ext[:, MASK_LANE : MASK_LANE + 1] > 0.5
    own = jnp.where(keep, own_ref[...].astype(F32), 0.0).astype(BF16)
    own_ref[...] = own
    edge_ref[...] = jnp.where(core_ref[0] == 0, own[0:HALO].astype(F32), own[ROWS - HALO :].astype(F32)).astype(BF16)


def split_body(core_ref, own_ref, halo_ref, ext_ref, out_ref, rows_ref, side_ref):
    own = own_ref[...]
    none = jnp.zeros((HALO, LANES), F32)

    @pl.when(core_ref[0] == 0)
    def _():
        rows_ref[0:HALO] = halo_ref[...]
        rows_ref[HALO:SENT] = own
        side_ref[0:HALO] = none
        side_ref[HALO:SENT] = ext_ref[...]

    @pl.when(core_ref[0] != 0)
    def _():
        rows_ref[0:ROWS] = own
        rows_ref[ROWS:SENT] = halo_ref[...]
        side_ref[0:ROWS] = ext_ref[...]
        side_ref[ROWS:SENT] = none

    ext = side_ref[...]
    permute = one_hot()
    width = 2 * D // Z
    for part in range(Z // 2):
        piece = rows_ref[:, part * width : (part + 1) * width]
        moved = jnp.dot(piece, permute, preferred_element_type=F32)
        for i in range(4):
            out_ref[4 * part + i] = (moved[:, i * LANES : (i + 1) * LANES] + ext).astype(BF16)


def lane_rows(x, lane):
    return jnp.broadcast_to(x[:, lane : lane + 1], x.shape)


def mask_rows(x):
    return lane_rows(x, MASK_LANE)


def near_rows(ref, base, offset, before, after):
    rows = ref[base + offset : base + offset + CHUNK]
    if offset == 0:
        return rows
    same = before >= -offset if offset < 0 else after >= offset
    return jnp.where(same, rows, 0.0)


def conv_body(
    x_ref, wp_ref, conv_ref, stat_ref, par_ref, w_ref, wide_ref,
    xf_ref, prev_ref, next_ref, tmp_ref, wf_ref, run_ref,
):
    step = pl.program_id(0)

    @pl.when(step == 0)
    def _():
        wf_ref[CHAN:] = jnp.zeros((LANES - CHAN, WIDE), F32)
        for d in range(SETS):
            wf_ref[d * OWN : (d + 1) * OWN] = wp_ref[d].astype(F32)
        wide = wf_ref[:, 0:D].astype(BF16)
        wide_ref[...] = wide
        w_ref[...] = wide[:CHAN]
        tmp_ref[...] = wf_ref[:, D:WIDE].T
        par_ref[...] = tmp_ref[0:PART] + tmp_ref[PART : 2 * PART] + tmp_ref[2 * PART : 3 * PART]
        run_ref[...] = jnp.zeros_like(run_ref)

    x = x_ref[0].astype(F32)
    xf_ref[...] = x
    inside = x[HALO : HALO + BLOCK]
    prev_ref[...] = lane_rows(inside, PREV_LANE)
    next_ref[...] = lane_rows(inside, NEXT_LANE)
    for chunk in range(BLOCK // CHUNK):
        at = slice(chunk * CHUNK, (chunk + 1) * CHUNK)
        before, after = prev_ref[at], next_ref[at]
        total = jnp.zeros((CHUNK, LANES), F32)
        for k in range(KERNEL):
            near = near_rows(xf_ref, HALO + chunk * CHUNK, k - HALF, before, after)
            total = total + par_ref[k : k + 1] * near
        conv_ref[0, at] = total

    rows = lambda v: jnp.sum(jnp.sum(v.reshape(-1, 8, LANES), axis=0), axis=0, keepdims=True)
    m = mask_rows(inside)
    conv = conv_ref[0]
    here = rows(m)
    mean_here = rows(m * conv) / here
    off = conv - mean_here
    count, mean, spread = run_ref[0:1], run_ref[1:2], run_ref[2:3]
    both = count + here
    apart = mean_here - mean
    run_ref[0:1] = both
    run_ref[1:2] = mean + apart * (here / both)
    run_ref[2:3] = spread + rows(m * off * off) + apart * apart * (count * here / both)

    @pl.when(step == Z - 1)
    def _():
        for d in range(SETS):
            stat_ref[d] = run_ref[...]


def moments(stat_ref):
    each = [stat_ref[d] for d in range(SETS)]
    count = sum(e[0:1] for e in each)
    mean = sum(e[0:1] * e[1:2] for e in each) / count
    spread = sum(e[2:3] for e in each)
    for e in each:
        off = e[1:2] - mean
        spread = spread + e[0:1] * off * off
    inv_std = lax.rsqrt(spread / count + 1e-05)
    return count, mean, inv_std


def grad_body(
    conv_ref, x_ref, wide_ref, par_ref, stat_ref, cot_hbm,
    act_ref, gp_ref, first_ref, last_ref, gw_ref,
    total_ref, acc_ref, mom_ref, cot_ref, sem,
):
    step = pl.program_id(0)

    def fetch(i):
        rows = pl.ds(i * CORES, CORES)
        return pltpu.make_async_copy(cot_hbm.at[rows], cot_ref.at[rows], sem.at[i])

    @pl.when(step == 0)
    def _():
        for i in range(Z):
            fetch(i).start()

    @pl.when(step == 0)
    def _():
        total_ref[...] = jnp.zeros_like(total_ref)
        acc_ref[...] = jnp.zeros_like(acc_ref)
        count, mean, inv_std = moments(stat_ref)
        mom_ref[0:1] = mean
        mom_ref[1:2] = inv_std

    mean, inv_std = mom_ref[0:1], mom_ref[1:2]
    m = mask_rows(x_ref[0, HALO : HALO + BLOCK].astype(F32))
    scale = par_ref[KERNEL : KERNEL + 1]
    shift = par_ref[KERNEL + 1 : KERNEL + 2]
    normed = (conv_ref[0] - mean) * inv_std
    pre = scale * normed + shift
    sig = jax.nn.sigmoid(pre)
    act = (m * pre * sig).astype(BF16)
    act_ref[0] = act[:ROWS]
    act_ref[1] = act[ROWS:]
    fetch(step).wait()
    cot = cot_ref[pl.ds(step * CORES, CORES)].reshape(BLOCK, D)
    grad_act = lax.dot_general(
        cot, wide_ref[...], (((1,), (1,)), ((), ())), preferred_element_type=F32
    )
    gp = m * grad_act * sig * (1.0 + pre * (1.0 - sig))
    nm = m * normed
    gp_ref[0] = gp
    lane = lax.broadcasted_iota(jnp.int32, (HALO, LANES), 1)
    for ref, at in ((first_ref, 0), (last_ref, BLOCK - HALO)):
        ref[0, 0] = gp[at : at + HALO].astype(BF16)
        ref[0, 1] = jnp.where(
            lane == MASK_LANE, m[at : at + HALO], nm[at : at + HALO]
        ).astype(BF16)

    acc_ref[0] += jnp.sum((gp * normed).reshape(-1, 8, LANES), axis=0)
    acc_ref[1] += jnp.sum(gp.reshape(-1, 8, LANES), axis=0)
    total_ref[...] += lax.dot_general(
        act, cot, (((0,), (0,)), ((), ())), preferred_element_type=F32
    )

    @pl.when(step == Z - 1)
    def _():
        sums = [jnp.sum(acc_ref[i], axis=0, keepdims=True) for i in range(2)]
        rows = jnp.concatenate(list(parts(sums[0])) + list(parts(sums[1])), axis=0).astype(BF16)
        for d in range(SETS):
            gw_ref[d, :, 0:D] = total_ref[d * OWN : (d + 1) * OWN].astype(BF16)
            gw_ref[d, :, D:WIDE] = rows


def back_body(
    set_ref, gp_ref, conv_ref, x_ref, act_ref, par_ref, stat_ref, sum_ref, left_ref, right_ref,
    pack_ref, taps_ref, sums_ref,
    gc_ref, xf_ref, prev_ref, next_ref, tap_ref, run_ref,
):
    b = pl.program_id(0)

    @pl.when(b == 0)
    def _():
        count, mean, inv_std = moments(stat_ref)
        each = sum_ref[0, :, D:WIDE].astype(F32)
        for d in range(1, SETS):
            each = each + sum_ref[d, :, D:WIDE].astype(F32)
        scale_sum = each[0:1] + each[1:2] + each[2:3]
        shift_sum = each[3:4] + each[4:5] + each[5:6]
        sums_ref[...] = jnp.concatenate([scale_sum, shift_sum, jnp.zeros((6, LANES), F32)], axis=0)
        run_ref[0:1] = par_ref[KERNEL : KERNEL + 1] * inv_std
        run_ref[1:2] = scale_sum / count
        run_ref[2:3] = shift_sum / count
        run_ref[3:4] = mean
        run_ref[4:5] = inv_std
        tap_ref[...] = jnp.zeros_like(tap_ref)

    gain, by_norm, by_one = run_ref[0:1], run_ref[1:2], run_ref[2:3]
    where_am_i = set_ref[0]

    def outside(ref, at):
        gp = ref[at, 0].astype(F32)
        nm = ref[at, 1].astype(F32)
        return gain * (gp - by_one * mask_rows(nm) - by_norm * nm)

    x = x_ref[0, HALO : HALO + BLOCK].astype(F32)
    xf_ref[...] = x
    prev_ref[...] = lane_rows(x, PREV_LANE)
    next_ref[...] = lane_rows(x, NEXT_LANE)
    gc_ref[0:HALO] = outside(left_ref, jnp.where(where_am_i == 0, jnp.maximum(b - 1, 0), b))
    gc_ref[HALO + BLOCK : SPAN] = outside(
        right_ref, jnp.where(where_am_i == SETS - 1, jnp.minimum(b + 1, Z - 1), b)
    )
    m = mask_rows(x)
    normed = (conv_ref[0] - run_ref[3:4]) * run_ref[4:5]
    gc_ref[HALO : HALO + BLOCK] = gain * (gp_ref[0] - m * (by_one + by_norm * normed))
    pieces = []
    for chunk in range(BLOCK // CHUNK):
        at = slice(chunk * CHUNK, (chunk + 1) * CHUNK)
        before, after, centre = prev_ref[at], next_ref[at], xf_ref[at]
        total = jnp.zeros((CHUNK, LANES), F32)
        for k in range(KERNEL):
            near = near_rows(gc_ref, HALO + chunk * CHUNK, HALF - k, before, after)
            total = total + par_ref[k : k + 1] * near
            tap_ref[k] += jnp.sum((centre * near).reshape(-1, 8, LANES), axis=0)
        pieces.append(total)
    for core in range(CORES):
        half = jnp.concatenate(
            pieces[core * (ROWS // CHUNK) : (core + 1) * (ROWS // CHUNK)], axis=0
        )
        half = half * m[core * ROWS : (core + 1) * ROWS]
        turned = pltpu.roll(half, CHAN, 1)
        lane = lax.broadcasted_iota(jnp.int32, (ROWS, LANES), 1)
        pack_ref[core, 0:ROWS] = jnp.where(
            lane < CHAN, act_ref[core].astype(F32), turned
        ).astype(BF16)
        lane = lane[: ROWS // 2]
        pack_ref[core, ROWS : ROWS + ROWS // 2] = jnp.where(
            lane < LANES // 2, turned[: ROWS // 2], pltpu.roll(turned[ROWS // 2 :], LANES // 2, 1)
        ).astype(BF16)

    @pl.when(b == Z - 1)
    def _():
        taps_ref[...] = jnp.sum(tap_ref[...], axis=1)


def join_body(pack_ref, w_ref, out_ref, gh_ref, four_ref, total_ref):
    step = pl.program_id(0)
    lane = lax.broadcasted_iota(jnp.int32, (ROWS // 2, LANES), 1)

    @pl.when(step == 0)
    def _():
        total_ref[...] = jnp.zeros_like(total_ref)

    total = total_ref[...]
    for i in range(4):
        main = pack_ref[i, 0:ROWS]
        total = total + jnp.dot(
            main[:, :CHAN], w_ref[i * CHAN : (i + 1) * CHAN], preferred_element_type=F32
        )
        main = main.astype(F32)
        rest = pack_ref[i, ROWS : ROWS + ROWS // 2].astype(F32)
        upper = jnp.where(lane < LANES // 2, rest, main[: ROWS // 2])
        lower = jnp.where(lane < LANES // 2, pltpu.roll(rest, LANES // 2, 1), main[ROWS // 2 :])
        turned = jnp.concatenate([upper, lower], axis=0)
        four_ref[:, i * LANES : (i + 1) * LANES] = pltpu.roll(turned, LANES - CHAN, 1).astype(BF16)
    total_ref[...] = total
    gh_ref[...] = lax.dot_general(
        four_ref[...], one_hot(), (((1,), (1,)), ((), ())), preferred_element_type=F32
    ).astype(BF16)

    @pl.when(step == Z // 2 - 1)
    def _():
        out_ref[...] = total.astype(BF16)


def shape(dims, kind):
    return jax.ShapeDtypeStruct(dims, kind)


def local(hidden_in, segment_ids, frame_mask, dw_kernel, norm_scale, norm_shift, out_weight, cotangent):
    core = lax.axis_index("core")
    here = lax.axis_index(ALL)
    this_set = lax.axis_index(OVER_SETS)

    with jax.named_scope("cotangent_of_group"):
        cot_all = lax.all_gather(cotangent, IN_GROUP)

    with jax.named_scope("prepare"):
        seg = lax.dynamic_slice_in_dim(
            jnp.pad(segment_ids, (HALO, LANES - HALO), constant_values=-1), here * ROWS, 2 * LANES
        )
        row = lambda v: v.reshape(1, -1)
        wp, ext, own, edge = call(
            prep_body,
            (
                shape((SETS, OWN, WIDE), BF16),
                shape((ROWS, LANES), F32),
                shape((ROWS, D), BF16),
                shape((HALO, D), BF16),
            ),
            (core.reshape(1), row(seg), dw_kernel.T, row(norm_scale), row(norm_shift), row(frame_mask), out_weight, hidden_in),
            [
                pltpu.VMEM((LANES, LANES), F32),
                pltpu.VMEM((OWN, KERNEL), F32),
                pltpu.VMEM((1, OWN), F32),
                pltpu.VMEM((1, OWN), F32),
                pltpu.VMEM((1, ROWS), jnp.int32),
                pltpu.VMEM((OWN, D), BF16),
                pltpu.SemaphoreType.DMA((6,)),
            ],
            "prepare",
            limit=64,
            in_specs=[smem(), vmem()] + [hbm()] * 6,
            out_specs=[vmem()] * 4,
        )

    with jax.named_scope("edge_frames"):
        last = Z * SETS * CORES - 1
        pairs = [(i, i + 1) for i in range(1, last, 2)] + [(i + 1, i) for i in range(1, last, 2)]
        halo = lax.ppermute(edge, ALL, pairs)

    with jax.named_scope("rows_and_params"):
        wp = lax.all_to_all(wp, OVER_SETS, 0, 0)

    with jax.named_scope("frames_to_channels"):
        frames = call(
            split_body,
            shape((GROUP, SENT, LANES), BF16),
            (core.reshape(1), own, halo, ext),
            [pltpu.VMEM((SENT, D), BF16), pltpu.VMEM((SENT, LANES), F32)],
            "split",
            limit=64,
            in_specs=[smem(), vmem(), vmem(), vmem()],
            out_specs=vmem(),
        )
        frames, wp = lax.optimization_barrier((frames, wp))
        x = lax.all_to_all(frames, IN_GROUP, 0, 0).reshape(Z, SPAN, LANES)

    whole = lambda *dims: pl.BlockSpec(dims, lambda i: (0,) * len(dims))
    each = lambda *dims: pl.BlockSpec(dims, lambda i: (i,) + (0,) * (len(dims) - 1))

    with jax.named_scope("conv"):
        conv, stat, par, rows, wide = call(
            conv_body,
            (
                shape((Z, BLOCK, LANES), F32),
                shape((SETS, 8, LANES), F32),
                shape((PART, LANES), F32),
                shape((CHAN, D), BF16),
                shape((LANES, D), BF16),
            ),
            (x, wp),
            [
                pltpu.VMEM((SPAN, LANES), F32),
                pltpu.VMEM((BLOCK, LANES), F32),
                pltpu.VMEM((BLOCK, LANES), F32),
                pltpu.VMEM((LANES, LANES), F32),
                pltpu.VMEM((LANES, WIDE), F32),
                pltpu.VMEM((8, LANES), F32),
            ],
            "conv",
            limit=24,
            work=6 * 10**9,
            grid=(Z,),
            in_specs=[each(1, SPAN, LANES), whole(SETS, OWN, WIDE)],
            out_specs=[
                each(1, BLOCK, LANES),
                whole(SETS, 8, LANES),
                whole(PART, LANES),
                whole(CHAN, D),
                whole(LANES, D),
            ],
        )

    with jax.named_scope("weights_of_group"):
        w_all = lax.all_gather(rows, IN_GROUP, tiled=True)

    with jax.named_scope("norm_sums"):
        stat = lax.all_to_all(stat, OVER_SETS, 0, 0)

    with jax.named_scope("activation_grad"):
        act, gp, first, last_rows, gw = call(
            grad_body,
            (
                shape((GROUP, ROWS, LANES), BF16),
                shape((Z, BLOCK, LANES), F32),
                shape((Z, 2, HALO, LANES), BF16),
                shape((Z, 2, HALO, LANES), BF16),
                shape((SETS, OWN, WIDE), BF16),
            ),
            (conv, x, wide, par, stat, cot_all),
            [
                pltpu.VMEM((LANES, D), F32),
                pltpu.VMEM((2, 8, LANES), F32),
                pltpu.VMEM((8, LANES), F32),
                pltpu.VMEM((GROUP, ROWS, D), BF16),
                pltpu.SemaphoreType.DMA((Z,)),
            ],
            "activation",
            limit=48,
            grid=(Z,),
            in_specs=[
                pl.BlockSpec((1, BLOCK, LANES), lambda i: (i, 0, 0)),
                pl.BlockSpec((1, SPAN, LANES), lambda i: (i, 0, 0)),
                whole(LANES, D),
                whole(PART, LANES),
                whole(SETS, 8, LANES),
                hbm(),
            ],
            out_specs=[
                pl.BlockSpec((CORES, ROWS, LANES), lambda i: (i, 0, 0)),
                pl.BlockSpec((1, BLOCK, LANES), lambda i: (i, 0, 0)),
                pl.BlockSpec((1, 2, HALO, LANES), lambda i: (i, 0, 0, 0)),
                pl.BlockSpec((1, 2, HALO, LANES), lambda i: (i, 0, 0, 0)),
                whole(SETS, OWN, WIDE),
            ],
        )

    with jax.named_scope("edge_grads"):
        up = [(i, (i + 1) % SETS) for i in range(SETS)]
        down = [((i + 1) % SETS, i) for i in range(SETS)]
        left = lax.ppermute(last_rows, OVER_SETS, up)
        right = lax.ppermute(first, OVER_SETS, down)

    with jax.named_scope("norm_grad_sums"):
        gw = lax.all_to_all(gw, OVER_SETS, 0, 0)

    with jax.named_scope("conv_grad"):
        pack, taps, both = call(
            back_body,
            (
                shape((GROUP, ROWS + ROWS // 2, LANES), BF16),
                shape((32, LANES), F32),
                shape((8, LANES), F32),
            ),
            (this_set.reshape(1), gp, conv, x, act, par, stat, gw, left, right),
            [
                pltpu.VMEM((SPAN, LANES), F32),
                pltpu.VMEM((BLOCK, LANES), F32),
                pltpu.VMEM((BLOCK, LANES), F32),
                pltpu.VMEM((BLOCK, LANES), F32),
                pltpu.VMEM((32, 8, LANES), F32),
                pltpu.VMEM((8, LANES), F32),
            ],
            "conv_grad",
            limit=24,
            work=10**10,
            grid=(Z,),
            in_specs=[
                smem(),
                each(1, BLOCK, LANES),
                each(1, BLOCK, LANES),
                each(1, SPAN, LANES),
                each(CORES, ROWS, LANES),
                whole(PART, LANES),
                whole(SETS, 8, LANES),
                whole(SETS, OWN, WIDE),
                whole(Z, 2, HALO, LANES),
                whole(Z, 2, HALO, LANES),
            ],
            out_specs=[each(CORES, ROWS + ROWS // 2, LANES), whole(32, LANES), whole(8, LANES)],
        )

    with jax.named_scope("channels_to_frames"):
        back = lax.all_to_all(pack, IN_GROUP, 0, 0)

    with jax.named_scope("sums_of_taps"):
        taps, w_all = lax.optimization_barrier((taps, w_all))
        for axis, size in (("x", X), ("y", Y)):
            moved = [
                lax.ppermute(taps, axis, [(i, (i + by) % size) for i in range(size)])
                for by in range(1, size)
            ]
            taps = taps + sum(moved)
        at = this_set * OWN
        grad_kernel = lax.dynamic_slice(taps, (0, at), (KERNEL, OWN))
        grad_scale = lax.dynamic_slice(both, (0, at), (1, OWN))[0]
        grad_shift = lax.dynamic_slice(both, (1, at), (1, OWN))[0]

    with jax.named_scope("weight_grad_sums"):
        grad_weight = jnp.sum(gw[:, :, :D].astype(F32), axis=0)

    with jax.named_scope("join"):
        width = 2 * D // Z
        module_out, grad_hidden = call(
            join_body,
            (shape((ROWS, D), BF16), shape((ROWS, D), BF16)),
            (back, w_all),
            [
                pltpu.VMEM((ROWS, 4 * LANES), BF16),
                pltpu.VMEM((ROWS, D), F32),
            ],
            "join",
            limit=24,
            grid=(Z // 2,),
            in_specs=[
                pl.BlockSpec((4, ROWS + ROWS // 2, LANES), lambda i: (i, 0, 0)),
                pl.BlockSpec((width, D), lambda i: (i, 0)),
            ],
            out_specs=[
                pl.BlockSpec((ROWS, D), lambda i: (0, 0)),
                pl.BlockSpec((ROWS, width), lambda i: (0, i)),
            ],
        )
    return (module_out, grad_hidden, grad_kernel, grad_scale, grad_shift, grad_weight)


def solution(mesh):
    grid = Mesh(mesh.devices.reshape(Z, X, Y, CORES), ALL)
    return jax.shard_map(
        local,
        mesh=grid,
        in_specs=(P(ALL, None), P(), P(ALL), P(None, ALL), P(ALL), P(ALL), P(ALL, None), P(ALL, None)),
        out_specs=(P(ALL, None), P(ALL, None), P(None, ALL), P(ALL), P(ALL), P(ALL, None)),
        check_vma=False,
    )
```

```python
import jax
import jax.numpy as jnp
from jax import lax
from jax.experimental import pallas as pl
from jax.experimental.pallas import tpu as pltpu
from jax.sharding import Mesh, PartitionSpec as P

Z, X, Y, CORES = 8, 4, 4, 2
GROUP = Z * CORES
SETS = X * Y
KERNEL = 31
HALF = KERNEL // 2
D = 1536
ROWS = 128
OWN = D // (GROUP * SETS)
CHAN = OWN * SETS
HALO = 16
LANES = 128
BLOCK = CORES * ROWS
SPAN = BLOCK + 2 * HALO
SENT = ROWS + HALO
CHUNK = 64
WIDE = D + LANES
PART = 40
MASK_LANE, PREV_LANE, NEXT_LANE = CHAN, CHAN + 1, CHAN + 2
ALL = ("z", "x", "y", "core")
IN_GROUP = ("z", "core")
OVER_SETS = ("x", "y")
F32, BF16 = jnp.float32, jnp.bfloat16


def call(body, outs, ins, scratch, name, limit=64, work=0, **more):
    if work:
        more["cost_estimate"] = pl.CostEstimate(flops=work, bytes_accessed=2**20, transcendentals=0)
    if scratch:
        more["scratch_shapes"] = scratch
    return pl.pallas_call(
        body,
        out_shape=outs,
        name=name,
        compiler_params=pltpu.CompilerParams(vmem_limit_bytes=limit * 2**20),
        **more,
    )(*ins)


def vmem():
    return pl.BlockSpec(memory_space=pltpu.VMEM)


def hbm():
    return pl.BlockSpec(memory_space=pltpu.HBM)


def parts(x):
    high = x.astype(BF16).astype(F32)
    mid = (x - high).astype(BF16).astype(F32)
    return high, mid, (x - high - mid).astype(BF16).astype(F32)


def smem():
    return pl.BlockSpec(memory_space=pltpu.SMEM)


def one_hot():
    col = lax.broadcasted_iota(jnp.int32, (1, 4 * LANES), 1)
    lane = col % LANES
    piece = col // LANES
    source = (
        (piece // 2) * (D // Z) + (lane // OWN) * (CORES * OWN) + (piece % 2) * OWN + lane % OWN
    )
    source = jnp.where(lane < CHAN, source, -1)
    row = lax.broadcasted_iota(jnp.int32, (2 * D // Z, 4 * LANES), 0)
    return jnp.where(row == source, 1.0, 0.0).astype(BF16)


def prep_body(
    core_ref, seg_ref, taps_hbm, scale_hbm, shift_hbm, mask_hbm, w_hbm, own_hbm,
    wp_ref, ext_ref, own_ref, edge_ref,
    tmp_ref, taps_ref, scale_ref, shift_ref, mask_ref, w_ref, sem,
):
    pairs = (
        (taps_hbm, taps_ref), (scale_hbm, scale_ref), (shift_hbm, shift_ref),
        (mask_hbm, mask_ref), (w_hbm, w_ref), (own_hbm, own_ref),
    )
    copies = [pltpu.make_async_copy(a, b, sem.at[i]) for i, (a, b) in enumerate(pairs)]
    for copy in copies:
        copy.start()
    tmp_ref[...] = jnp.zeros_like(tmp_ref)
    for copy in copies:
        copy.wait()
    tmp_ref[KERNEL : KERNEL + 1, 0:OWN] = scale_ref[...]
    tmp_ref[KERNEL + 1 : KERNEL + 2, 0:OWN] = shift_ref[...]
    rows = tmp_ref[...].T
    tmp_ref[0:8] = rows[0:8]
    tmp_ref[0:OWN, 0:KERNEL] = taps_ref[...]
    high, mid, low = parts(tmp_ref[0:8])
    side = high + pltpu.roll(mid, PART, 1) + pltpu.roll(low, 2 * PART, 1)
    side = side[0:OWN].astype(BF16)
    for d in range(SETS):
        wp_ref[d, :, 0:D] = w_ref[...]
        wp_ref[d, :, D:WIDE] = side
    seg = seg_ref[...]
    own = seg[:, HALO : HALO + ROWS]
    before = jnp.zeros((1, ROWS), F32)
    after = jnp.zeros((1, ROWS), F32)
    for j in range(1, HALF + 1):
        before = before + jnp.where(seg[:, HALO - j : HALO - j + ROWS] == own, 1.0, 0.0)
        after = after + jnp.where(seg[:, HALO + j : HALO + j + ROWS] == own, 1.0, 0.0)
    tmp_ref[...] = jnp.zeros_like(tmp_ref)
    tmp_ref[MASK_LANE : MASK_LANE + 1] = mask_ref[...].astype(F32)
    tmp_ref[PREV_LANE : PREV_LANE + 1] = before
    tmp_ref[NEXT_LANE : NEXT_LANE + 1] = after
    ext = tmp_ref[...].T
    ext_ref[...] = ext
    keep = ext[:, MASK_LANE : MASK_LANE + 1] > 0.5
    own = jnp.where(keep, own_ref[...].astype(F32), 0.0).astype(BF16)
    own_ref[...] = own
    edge_ref[...] = jnp.where(core_ref[0] == 0, own[0:HALO].astype(F32), own[ROWS - HALO :].astype(F32)).astype(BF16)


def split_body(core_ref, own_ref, halo_ref, ext_ref, out_ref, rows_ref, side_ref):
    own = own_ref[...]
    none = jnp.zeros((HALO, LANES), F32)

    @pl.when(core_ref[0] == 0)
    def _():
        rows_ref[0:HALO] = halo_ref[...]
        rows_ref[HALO:SENT] = own
        side_ref[0:HALO] = none
        side_ref[HALO:SENT] = ext_ref[...]

    @pl.when(core_ref[0] != 0)
    def _():
        rows_ref[0:ROWS] = own
        rows_ref[ROWS:SENT] = halo_ref[...]
        side_ref[0:ROWS] = ext_ref[...]
        side_ref[ROWS:SENT] = none

    ext = side_ref[...]
    permute = one_hot()
    width = 2 * D // Z
    for part in range(Z // 2):
        piece = rows_ref[:, part * width : (part + 1) * width]
        moved = jnp.dot(piece, permute, preferred_element_type=F32)
        for i in range(4):
            out_ref[4 * part + i] = (moved[:, i * LANES : (i + 1) * LANES] + ext).astype(BF16)


def lane_rows(x, lane):
    return jnp.broadcast_to(x[:, lane : lane + 1], x.shape)


def mask_rows(x):
    return lane_rows(x, MASK_LANE)


def near_rows(ref, base, offset, before, after):
    rows = ref[base + offset : base + offset + CHUNK]
    if offset == 0:
        return rows
    same = before >= -offset if offset < 0 else after >= offset
    return jnp.where(same, rows, 0.0)


def rows_body(wp_ref, par_ref, w_ref, wide_ref, tmp_ref, wf_ref):
    wf_ref[CHAN:] = jnp.zeros((LANES - CHAN, WIDE), F32)
    for d in range(SETS):
        wf_ref[d * OWN : (d + 1) * OWN] = wp_ref[d].astype(F32)
    wide = wf_ref[:, 0:D].astype(BF16)
    wide_ref[...] = wide
    w_ref[...] = wide[:CHAN]
    tmp_ref[...] = wf_ref[:, D:WIDE].T
    par_ref[...] = tmp_ref[0:PART] + tmp_ref[PART : 2 * PART] + tmp_ref[2 * PART : 3 * PART]


def conv_body(
    x_ref, par_ref, conv_ref, stat_ref, xf_ref, prev_ref, next_ref, run_ref
):
    step = pl.program_id(0)

    @pl.when(step == 0)
    def _():
        run_ref[...] = jnp.zeros_like(run_ref)

    x = x_ref[0].astype(F32)
    xf_ref[...] = x
    inside = x[HALO : HALO + BLOCK]
    prev_ref[...] = lane_rows(inside, PREV_LANE)
    next_ref[...] = lane_rows(inside, NEXT_LANE)
    for chunk in range(BLOCK // CHUNK):
        at = slice(chunk * CHUNK, (chunk + 1) * CHUNK)
        before, after = prev_ref[at], next_ref[at]
        total = jnp.zeros((CHUNK, LANES), F32)
        for k in range(KERNEL):
            near = near_rows(xf_ref, HALO + chunk * CHUNK, k - HALF, before, after)
            total = total + par_ref[k : k + 1] * near
        conv_ref[0, at] = total

    rows = lambda v: jnp.sum(jnp.sum(v.reshape(-1, 8, LANES), axis=0), axis=0, keepdims=True)
    m = mask_rows(inside)
    conv = conv_ref[0]
    here = rows(m)
    mean_here = rows(m * conv) / here
    off = conv - mean_here
    count, mean, spread = run_ref[0:1], run_ref[1:2], run_ref[2:3]
    both = count + here
    apart = mean_here - mean
    run_ref[0:1] = both
    run_ref[1:2] = mean + apart * (here / both)
    run_ref[2:3] = spread + rows(m * off * off) + apart * apart * (count * here / both)

    @pl.when(step == Z - 1)
    def _():
        for d in range(SETS):
            stat_ref[d] = run_ref[...]


def moments(stat_ref):
    each = [stat_ref[d] for d in range(SETS)]
    count = sum(e[0:1] for e in each)
    mean = sum(e[0:1] * e[1:2] for e in each) / count
    spread = sum(e[2:3] for e in each)
    for e in each:
        off = e[1:2] - mean
        spread = spread + e[0:1] * off * off
    inv_std = lax.rsqrt(spread / count + 1e-05)
    return count, mean, inv_std


def grad_body(
    conv_ref, x_ref, wide_ref, par_ref, stat_ref, cot_hbm,
    act_ref, gp_ref, first_ref, last_ref, gw_ref,
    total_ref, acc_ref, mom_ref, cot_ref, sem,
):
    step = pl.program_id(0)

    def fetch(i):
        rows = pl.ds(i * CORES, CORES)
        return pltpu.make_async_copy(cot_hbm.at[rows], cot_ref.at[rows], sem.at[i])

    @pl.when(step == 0)
    def _():
        for i in range(Z):
            fetch(i).start()

    @pl.when(step == 0)
    def _():
        total_ref[...] = jnp.zeros_like(total_ref)
        acc_ref[...] = jnp.zeros_like(acc_ref)
        count, mean, inv_std = moments(stat_ref)
        mom_ref[0:1] = mean
        mom_ref[1:2] = inv_std

    mean, inv_std = mom_ref[0:1], mom_ref[1:2]
    m = mask_rows(x_ref[0, HALO : HALO + BLOCK].astype(F32))
    scale = par_ref[KERNEL : KERNEL + 1]
    shift = par_ref[KERNEL + 1 : KERNEL + 2]
    normed = (conv_ref[0] - mean) * inv_std
    pre = scale * normed + shift
    sig = jax.nn.sigmoid(pre)
    act = (m * pre * sig).astype(BF16)
    act_ref[0] = act[:ROWS]
    act_ref[1] = act[ROWS:]
    fetch(step).wait()
    cot = cot_ref[pl.ds(step * CORES, CORES)].reshape(BLOCK, D)
    grad_act = lax.dot_general(
        cot, wide_ref[...], (((1,), (1,)), ((), ())), preferred_element_type=F32
    )
    gp = m * grad_act * sig * (1.0 + pre * (1.0 - sig))
    nm = m * normed
    gp_ref[0] = gp
    lane = lax.broadcasted_iota(jnp.int32, (HALO, LANES), 1)
    for ref, at in ((first_ref, 0), (last_ref, BLOCK - HALO)):
        ref[0, 0] = gp[at : at + HALO].astype(BF16)
        ref[0, 1] = jnp.where(
            lane == MASK_LANE, m[at : at + HALO], nm[at : at + HALO]
        ).astype(BF16)

    acc_ref[0] += jnp.sum((gp * normed).reshape(-1, 8, LANES), axis=0)
    acc_ref[1] += jnp.sum(gp.reshape(-1, 8, LANES), axis=0)
    total_ref[...] += lax.dot_general(
        act, cot, (((0,), (0,)), ((), ())), preferred_element_type=F32
    )

    @pl.when(step == Z - 1)
    def _():
        sums = [jnp.sum(acc_ref[i], axis=0, keepdims=True) for i in range(2)]
        rows = jnp.concatenate(list(parts(sums[0])) + list(parts(sums[1])), axis=0).astype(BF16)
        for d in range(SETS):
            gw_ref[d, :, 0:D] = total_ref[d * OWN : (d + 1) * OWN].astype(BF16)
            gw_ref[d, :, D:WIDE] = rows


def back_body(
    set_ref, gp_ref, conv_ref, x_ref, par_ref, stat_ref, sum_ref, left_ref, right_ref,
    pack_ref, taps_ref, sums_ref,
    gc_ref, xf_ref, prev_ref, next_ref, tap_ref, run_ref,
):
    b = pl.program_id(0)

    @pl.when(b == 0)
    def _():
        count, mean, inv_std = moments(stat_ref)
        each = sum_ref[0, :, D:WIDE].astype(F32)
        for d in range(1, SETS):
            each = each + sum_ref[d, :, D:WIDE].astype(F32)
        scale_sum = each[0:1] + each[1:2] + each[2:3]
        shift_sum = each[3:4] + each[4:5] + each[5:6]
        sums_ref[...] = jnp.concatenate([scale_sum, shift_sum, jnp.zeros((6, LANES), F32)], axis=0)
        run_ref[0:1] = par_ref[KERNEL : KERNEL + 1] * inv_std
        run_ref[1:2] = scale_sum / count
        run_ref[2:3] = shift_sum / count
        run_ref[3:4] = mean
        run_ref[4:5] = inv_std
        tap_ref[...] = jnp.zeros_like(tap_ref)

    gain, by_norm, by_one = run_ref[0:1], run_ref[1:2], run_ref[2:3]
    where_am_i = set_ref[0]

    def outside(ref, at):
        gp = ref[at, 0].astype(F32)
        nm = ref[at, 1].astype(F32)
        return gain * (gp - by_one * mask_rows(nm) - by_norm * nm)

    x = x_ref[0, HALO : HALO + BLOCK].astype(F32)
    xf_ref[...] = x
    prev_ref[...] = lane_rows(x, PREV_LANE)
    next_ref[...] = lane_rows(x, NEXT_LANE)
    gc_ref[0:HALO] = outside(left_ref, jnp.where(where_am_i == 0, jnp.maximum(b - 1, 0), b))
    gc_ref[HALO + BLOCK : SPAN] = outside(
        right_ref, jnp.where(where_am_i == SETS - 1, jnp.minimum(b + 1, Z - 1), b)
    )
    m = mask_rows(x)
    normed = (conv_ref[0] - run_ref[3:4]) * run_ref[4:5]
    gc_ref[HALO : HALO + BLOCK] = gain * (gp_ref[0] - m * (by_one + by_norm * normed))
    pieces = []
    for chunk in range(BLOCK // CHUNK):
        at = slice(chunk * CHUNK, (chunk + 1) * CHUNK)
        before, after, centre = prev_ref[at], next_ref[at], xf_ref[at]
        total = jnp.zeros((CHUNK, LANES), F32)
        for k in range(KERNEL):
            near = near_rows(gc_ref, HALO + chunk * CHUNK, HALF - k, before, after)
            total = total + par_ref[k : k + 1] * near
            tap_ref[k] += jnp.sum((centre * near).reshape(-1, 8, LANES), axis=0)
        pieces.append(total)
    for core in range(CORES):
        half = jnp.concatenate(
            pieces[core * (ROWS // CHUNK) : (core + 1) * (ROWS // CHUNK)], axis=0
        )
        half = half * m[core * ROWS : (core + 1) * ROWS]
        pack_ref[core] = half.astype(BF16)

    @pl.when(b == Z - 1)
    def _():
        taps_ref[...] = jnp.sum(tap_ref[...], axis=1)


def out_body(act_ref, w_ref, out_ref):
    total = jnp.zeros((ROWS, D), F32)
    for at in range(GROUP):
        total = total + jnp.dot(
            act_ref[at][:, :CHAN], w_ref[at * CHAN : (at + 1) * CHAN], preferred_element_type=F32
        )
    out_ref[...] = total.astype(BF16)


def join_body(back_ref, gh_ref, four_ref):
    width = 4 * CHAN
    permute = one_hot()
    for part in range(Z // 2):
        for i in range(4):
            four_ref[:, i * LANES : (i + 1) * LANES] = back_ref[4 * part + i]
        gh_ref[:, part * width : (part + 1) * width] = lax.dot_general(
            four_ref[...], permute, (((1,), (1,)), ((), ())), preferred_element_type=F32
        ).astype(BF16)


def shape(dims, kind):
    return jax.ShapeDtypeStruct(dims, kind)


def local(hidden_in, segment_ids, frame_mask, dw_kernel, norm_scale, norm_shift, out_weight, cotangent):
    core = lax.axis_index("core")
    here = lax.axis_index(ALL)
    this_set = lax.axis_index(OVER_SETS)

    with jax.named_scope("cotangent_of_group"):
        cot_all = lax.all_gather(cotangent, IN_GROUP)

    with jax.named_scope("prepare"):
        seg = lax.dynamic_slice_in_dim(
            jnp.pad(segment_ids, (HALO, LANES - HALO), constant_values=-1), here * ROWS, 2 * LANES
        )
        row = lambda v: v.reshape(1, -1)
        wp, ext, own, edge = call(
            prep_body,
            (
                shape((SETS, OWN, WIDE), BF16),
                shape((ROWS, LANES), F32),
                shape((ROWS, D), BF16),
                shape((HALO, D), BF16),
            ),
            (core.reshape(1), row(seg), dw_kernel.T, row(norm_scale), row(norm_shift), row(frame_mask), out_weight, hidden_in),
            [
                pltpu.VMEM((LANES, LANES), F32),
                pltpu.VMEM((OWN, KERNEL), F32),
                pltpu.VMEM((1, OWN), F32),
                pltpu.VMEM((1, OWN), F32),
                pltpu.VMEM((1, ROWS), jnp.int32),
                pltpu.VMEM((OWN, D), BF16),
                pltpu.SemaphoreType.DMA((6,)),
            ],
            "prepare",
            limit=64,
            in_specs=[smem(), vmem()] + [hbm()] * 6,
            out_specs=[vmem()] * 4,
        )

    with jax.named_scope("edge_frames"):
        last = Z * SETS * CORES - 1
        pairs = [(i, i + 1) for i in range(1, last, 2)] + [(i + 1, i) for i in range(1, last, 2)]
        halo = lax.ppermute(edge, ALL, pairs)

    with jax.named_scope("rows_and_params"):
        wp = lax.all_to_all(wp, OVER_SETS, 0, 0)

    with jax.named_scope("frames_to_channels"):
        frames = call(
            split_body,
            shape((GROUP, SENT, LANES), BF16),
            (core.reshape(1), own, halo, ext),
            [pltpu.VMEM((SENT, D), BF16), pltpu.VMEM((SENT, LANES), F32)],
            "split",
            limit=64,
            in_specs=[smem(), vmem(), vmem(), vmem()],
            out_specs=vmem(),
        )
        frames, wp = lax.optimization_barrier((frames, wp))
        x = lax.all_to_all(frames, IN_GROUP, 0, 0).reshape(Z, SPAN, LANES)

    whole = lambda *dims: pl.BlockSpec(dims, lambda i: (0,) * len(dims))
    each = lambda *dims: pl.BlockSpec(dims, lambda i: (i,) + (0,) * (len(dims) - 1))

    with jax.named_scope("unpack_rows"):
        par, rows, wide = call(
            rows_body,
            (shape((PART, LANES), F32), shape((CHAN, D), BF16), shape((LANES, D), BF16)),
            (wp,),
            [pltpu.VMEM((LANES, LANES), F32), pltpu.VMEM((LANES, WIDE), F32)],
            "rows",
            limit=24,
            work=2 * 10**9,
            in_specs=[vmem()],
            out_specs=[vmem()] * 3,
        )

    with jax.named_scope("conv"):
        conv, stat = call(
            conv_body,
            (shape((Z, BLOCK, LANES), F32), shape((SETS, 8, LANES), F32)),
            (x, par),
            [
                pltpu.VMEM((SPAN, LANES), F32),
                pltpu.VMEM((BLOCK, LANES), F32),
                pltpu.VMEM((BLOCK, LANES), F32),
                pltpu.VMEM((8, LANES), F32),
            ],
            "conv",
            limit=24,
            work=6 * 10**9,
            grid=(Z,),
            in_specs=[each(1, SPAN, LANES), whole(PART, LANES)],
            out_specs=[each(1, BLOCK, LANES), whole(SETS, 8, LANES)],
        )

    with jax.named_scope("weights_of_group"):
        rows, conv = lax.optimization_barrier((rows, conv))
        w_all = lax.all_gather(rows, IN_GROUP, tiled=True)

    with jax.named_scope("norm_sums"):
        stat = lax.all_to_all(stat, OVER_SETS, 0, 0)

    with jax.named_scope("activation_grad"):
        act, gp, first, last_rows, gw = call(
            grad_body,
            (
                shape((GROUP, ROWS, LANES), BF16),
                shape((Z, BLOCK, LANES), F32),
                shape((Z, 2, HALO, LANES), BF16),
                shape((Z, 2, HALO, LANES), BF16),
                shape((SETS, OWN, WIDE), BF16),
            ),
            (conv, x, wide, par, stat, cot_all),
            [
                pltpu.VMEM((LANES, D), F32),
                pltpu.VMEM((2, 8, LANES), F32),
                pltpu.VMEM((8, LANES), F32),
                pltpu.VMEM((GROUP, ROWS, D), BF16),
                pltpu.SemaphoreType.DMA((Z,)),
            ],
            "activation",
            limit=48,
            grid=(Z,),
            in_specs=[
                pl.BlockSpec((1, BLOCK, LANES), lambda i: (i, 0, 0)),
                pl.BlockSpec((1, SPAN, LANES), lambda i: (i, 0, 0)),
                whole(LANES, D),
                whole(PART, LANES),
                whole(SETS, 8, LANES),
                hbm(),
            ],
            out_specs=[
                pl.BlockSpec((CORES, ROWS, LANES), lambda i: (i, 0, 0)),
                pl.BlockSpec((1, BLOCK, LANES), lambda i: (i, 0, 0)),
                pl.BlockSpec((1, 2, HALO, LANES), lambda i: (i, 0, 0, 0)),
                pl.BlockSpec((1, 2, HALO, LANES), lambda i: (i, 0, 0, 0)),
                whole(SETS, OWN, WIDE),
            ],
        )

    with jax.named_scope("edge_grads"):
        up = [(i, (i + 1) % SETS) for i in range(SETS)]
        down = [((i + 1) % SETS, i) for i in range(SETS)]
        left = lax.ppermute(last_rows, OVER_SETS, up)
        right = lax.ppermute(first, OVER_SETS, down)

    with jax.named_scope("norm_grad_sums"):
        gw = lax.all_to_all(gw, OVER_SETS, 0, 0)

    with jax.named_scope("act_to_frames"):
        act, gw = lax.optimization_barrier((act, gw))
        act = lax.all_to_all(act, IN_GROUP, 0, 0)

    with jax.named_scope("conv_grad"):
        pack, taps, both = call(
            back_body,
            (
                shape((GROUP, ROWS, LANES), BF16),
                shape((32, LANES), F32),
                shape((8, LANES), F32),
            ),
            (this_set.reshape(1), gp, conv, x, par, stat, gw, left, right),
            [
                pltpu.VMEM((SPAN, LANES), F32),
                pltpu.VMEM((BLOCK, LANES), F32),
                pltpu.VMEM((BLOCK, LANES), F32),
                pltpu.VMEM((BLOCK, LANES), F32),
                pltpu.VMEM((32, 8, LANES), F32),
                pltpu.VMEM((8, LANES), F32),
            ],
            "conv_grad",
            limit=24,
            work=10**10,
            grid=(Z,),
            in_specs=[
                smem(),
                each(1, BLOCK, LANES),
                each(1, BLOCK, LANES),
                each(1, SPAN, LANES),
                whole(PART, LANES),
                whole(SETS, 8, LANES),
                whole(SETS, OWN, WIDE),
                whole(Z, 2, HALO, LANES),
                whole(Z, 2, HALO, LANES),
            ],
            out_specs=[each(CORES, ROWS, LANES), whole(32, LANES), whole(8, LANES)],
        )

    with jax.named_scope("channels_to_frames"):
        back = lax.all_to_all(pack, IN_GROUP, 0, 0)

    with jax.named_scope("module_out"):
        taps, w_all, act = lax.optimization_barrier((taps, w_all, act))
        module_out = call(
            out_body,
            shape((ROWS, D), BF16),
            (act, w_all),
            [],
            "module_out",
            limit=24,
            work=4 * 10**9,
            in_specs=[vmem()] * 2,
            out_specs=vmem(),
        )

    with jax.named_scope("sums_of_taps"):
        for axis, size in (("x", X), ("y", Y)):
            moved = [
                lax.ppermute(taps, axis, [(i, (i + by) % size) for i in range(size)])
                for by in range(1, size)
            ]
            *moved, module_out = lax.optimization_barrier((*moved, module_out))
            taps = taps + sum(moved)
        at = this_set * OWN
        grad_kernel = lax.dynamic_slice(taps, (0, at), (KERNEL, OWN))
        grad_scale = lax.dynamic_slice(both, (0, at), (1, OWN))[0]
        grad_shift = lax.dynamic_slice(both, (1, at), (1, OWN))[0]

    with jax.named_scope("weight_grad_sums"):
        grad_weight = jnp.sum(gw[:, :, :D].astype(F32), axis=0)

    with jax.named_scope("join"):
        grad_hidden = call(
            join_body,
            shape((ROWS, D), BF16),
            (back,),
            [pltpu.VMEM((ROWS, 4 * LANES), BF16)],
            "join",
            limit=24,
            in_specs=[vmem()],
            out_specs=vmem(),
        )
    return (module_out, grad_hidden, grad_kernel, grad_scale, grad_shift, grad_weight)


def solution(mesh):
    grid = Mesh(mesh.devices.reshape(Z, X, Y, CORES), ALL)
    return jax.shard_map(
        local,
        mesh=grid,
        in_specs=(P(ALL, None), P(), P(ALL), P(None, ALL), P(ALL), P(ALL), P(ALL, None), P(ALL, None)),
        out_specs=(P(ALL, None), P(ALL, None), P(None, ALL), P(ALL), P(ALL), P(ALL, None)),
        check_vma=False,
    )
```

```python
import jax
import jax.numpy as jnp
from jax import lax
from jax.experimental import pallas as pl
from jax.experimental.pallas import tpu as pltpu
from jax.sharding import Mesh, PartitionSpec as P

Z, X, Y, CORES = 8, 4, 4, 2
GROUP = Z * CORES
SETS = X * Y
KERNEL = 31
HALF = KERNEL // 2
D = 1536
ROWS = 128
OWN = D // (GROUP * SETS)
CHAN = OWN * SETS
HALO = 16
LANES = 128
BLOCK = CORES * ROWS
SPAN = BLOCK + 2 * HALO
SENT = ROWS + HALO
CHUNK = 64
WIDE = D + LANES
PART = 40
GA = 48
MASK_LANE, PREV_LANE, NEXT_LANE = CHAN, CHAN + 1, CHAN + 2
ALL = ("z", "x", "y", "core")
IN_GROUP = ("z", "core")
OVER_SETS = ("x", "y")
F32, BF16 = jnp.float32, jnp.bfloat16


def call(body, outs, ins, scratch, name, limit=64, work=0, **more):
    if work:
        more["cost_estimate"] = pl.CostEstimate(flops=work, bytes_accessed=2**20, transcendentals=0)
    if scratch:
        more["scratch_shapes"] = scratch
    return pl.pallas_call(
        body,
        out_shape=outs,
        name=name,
        compiler_params=pltpu.CompilerParams(vmem_limit_bytes=limit * 2**20),
        **more,
    )(*ins)


def vmem():
    return pl.BlockSpec(memory_space=pltpu.VMEM)


def hbm():
    return pl.BlockSpec(memory_space=pltpu.HBM)


def parts(x):
    high = x.astype(BF16).astype(F32)
    mid = (x - high).astype(BF16).astype(F32)
    return high, mid, (x - high - mid).astype(BF16).astype(F32)


def smem():
    return pl.BlockSpec(memory_space=pltpu.SMEM)


def one_hot():
    col = lax.broadcasted_iota(jnp.int32, (1, 4 * LANES), 1)
    lane = col % LANES
    piece = col // LANES
    source = (
        (piece // 2) * (D // Z) + (lane // OWN) * (CORES * OWN) + (piece % 2) * OWN + lane % OWN
    )
    source = jnp.where(lane < CHAN, source, -1)
    row = lax.broadcasted_iota(jnp.int32, (2 * D // Z, 4 * LANES), 0)
    return jnp.where(row == source, 1.0, 0.0).astype(BF16)


def prep_body(
    core_ref, seg_ref, taps_hbm, scale_hbm, shift_hbm, mask_hbm, w_hbm, own_hbm,
    wp_ref, ext_ref, own_ref, edge_ref,
    tmp_ref, taps_ref, scale_ref, shift_ref, mask_ref, w_ref, sem,
):
    pairs = (
        (taps_hbm, taps_ref), (scale_hbm, scale_ref), (shift_hbm, shift_ref),
        (mask_hbm, mask_ref), (w_hbm, w_ref), (own_hbm, own_ref),
    )
    copies = [pltpu.make_async_copy(a, b, sem.at[i]) for i, (a, b) in enumerate(pairs)]
    for copy in copies:
        copy.start()
    tmp_ref[...] = jnp.zeros_like(tmp_ref)
    for copy in copies:
        copy.wait()
    tmp_ref[KERNEL : KERNEL + 1, 0:OWN] = scale_ref[...]
    tmp_ref[KERNEL + 1 : KERNEL + 2, 0:OWN] = shift_ref[...]
    rows = tmp_ref[...].T
    tmp_ref[0:8] = rows[0:8]
    tmp_ref[0:OWN, 0:KERNEL] = taps_ref[...]
    high, mid, low = parts(tmp_ref[0:8])
    side = high + pltpu.roll(mid, PART, 1) + pltpu.roll(low, 2 * PART, 1)
    side = side[0:OWN].astype(BF16)
    for d in range(SETS):
        wp_ref[d, :, 0:D] = w_ref[...]
        wp_ref[d, :, D:WIDE] = side
    seg = seg_ref[...]
    own = seg[:, HALO : HALO + ROWS]
    before = jnp.zeros((1, ROWS), F32)
    after = jnp.zeros((1, ROWS), F32)
    for j in range(1, HALF + 1):
        before = before + jnp.where(seg[:, HALO - j : HALO - j + ROWS] == own, 1.0, 0.0)
        after = after + jnp.where(seg[:, HALO + j : HALO + j + ROWS] == own, 1.0, 0.0)
    tmp_ref[...] = jnp.zeros_like(tmp_ref)
    tmp_ref[MASK_LANE : MASK_LANE + 1] = mask_ref[...].astype(F32)
    tmp_ref[PREV_LANE : PREV_LANE + 1] = before
    tmp_ref[NEXT_LANE : NEXT_LANE + 1] = after
    ext = tmp_ref[...].T
    ext_ref[...] = ext
    keep = ext[:, MASK_LANE : MASK_LANE + 1] > 0.5
    own = jnp.where(keep, own_ref[...].astype(F32), 0.0).astype(BF16)
    own_ref[...] = own
    edge_ref[...] = jnp.where(core_ref[0] == 0, own[0:HALO].astype(F32), own[ROWS - HALO :].astype(F32)).astype(BF16)


def split_body(core_ref, own_ref, halo_ref, ext_ref, out_ref, rows_ref, side_ref):
    own = own_ref[...]
    none = jnp.zeros((HALO, LANES), F32)

    @pl.when(core_ref[0] == 0)
    def _():
        rows_ref[0:HALO] = halo_ref[...]
        rows_ref[HALO:SENT] = own
        side_ref[0:HALO] = none
        side_ref[HALO:SENT] = ext_ref[...]

    @pl.when(core_ref[0] != 0)
    def _():
        rows_ref[0:ROWS] = own
        rows_ref[ROWS:SENT] = halo_ref[...]
        side_ref[0:ROWS] = ext_ref[...]
        side_ref[ROWS:SENT] = none

    ext = side_ref[...]
    permute = one_hot()
    width = 2 * D // Z
    for part in range(Z // 2):
        piece = rows_ref[:, part * width : (part + 1) * width]
        moved = jnp.dot(piece, permute, preferred_element_type=F32)
        for i in range(4):
            out_ref[4 * part + i] = (moved[:, i * LANES : (i + 1) * LANES] + ext).astype(BF16)


def lane_rows(x, lane):
    return jnp.broadcast_to(x[:, lane : lane + 1], x.shape)


def mask_rows(x):
    return lane_rows(x, MASK_LANE)


def near_rows(ref, base, offset, before, after):
    rows = ref[base + offset : base + offset + CHUNK]
    if offset == 0:
        return rows
    same = before >= -offset if offset < 0 else after >= offset
    return jnp.where(same, rows, 0.0)


def rows_body(wp_ref, par_ref, w_ref, wide_ref, tmp_ref, wf_ref):
    wf_ref[CHAN:] = jnp.zeros((LANES - CHAN, WIDE), F32)
    for d in range(SETS):
        wf_ref[d * OWN : (d + 1) * OWN] = wp_ref[d].astype(F32)
    wide = wf_ref[:, 0:D].astype(BF16)
    wide_ref[...] = wide
    w_ref[...] = wide[:CHAN]
    tmp_ref[...] = wf_ref[:, D:WIDE].T
    par_ref[...] = tmp_ref[0:PART] + tmp_ref[PART : 2 * PART] + tmp_ref[2 * PART : 3 * PART]


def conv_body(
    x_ref, par_ref, conv_ref, stat_ref, xf_ref, prev_ref, next_ref, run_ref
):
    step = pl.program_id(0)

    @pl.when(step == 0)
    def _():
        run_ref[...] = jnp.zeros_like(run_ref)

    x = x_ref[0].astype(F32)
    xf_ref[...] = x
    inside = x[HALO : HALO + BLOCK]
    prev_ref[...] = lane_rows(inside, PREV_LANE)
    next_ref[...] = lane_rows(inside, NEXT_LANE)
    for chunk in range(BLOCK // CHUNK):
        at = slice(chunk * CHUNK, (chunk + 1) * CHUNK)
        before, after = prev_ref[at], next_ref[at]
        total = jnp.zeros((CHUNK, LANES), F32)
        for k in range(KERNEL):
            near = near_rows(xf_ref, HALO + chunk * CHUNK, k - HALF, before, after)
            total = total + par_ref[k : k + 1] * near
        conv_ref[0, at] = total

    rows = lambda v: jnp.sum(jnp.sum(v.reshape(-1, 8, LANES), axis=0), axis=0, keepdims=True)
    m = mask_rows(inside)
    conv = conv_ref[0]
    here = rows(m)
    mean_here = rows(m * conv) / here
    off = conv - mean_here
    count, mean, spread = run_ref[0:1], run_ref[1:2], run_ref[2:3]
    both = count + here
    apart = mean_here - mean
    run_ref[0:1] = both
    run_ref[1:2] = mean + apart * (here / both)
    run_ref[2:3] = spread + rows(m * off * off) + apart * apart * (count * here / both)

    @pl.when(step == Z - 1)
    def _():
        for d in range(SETS):
            stat_ref[d] = run_ref[...]


def fold(x):
    tail = x[CHAN:]
    lane = lax.broadcasted_iota(jnp.int32, tail.shape, 1)
    size = LANES - CHAN
    return jnp.concatenate(
        [
            jnp.where(lane < CHAN, x[g * size : (g + 1) * size], pltpu.roll(tail, CHAN - g * size, 1))
            for g in range(CHAN // size)
        ],
        axis=0,
    )


def unfold(x):
    size = LANES - CHAN
    lane = lax.broadcasted_iota(jnp.int32, (size, LANES), 1)
    tail = jnp.zeros((size, LANES), F32)
    for g in range(CHAN // size):
        turned = pltpu.roll(x[g * size : (g + 1) * size], (g + 1) * size, 1)
        tail = jnp.where((lane >= g * size) & (lane < (g + 1) * size), turned, tail)
    return jnp.concatenate([x, tail], axis=0)


def moments(stat_ref):
    each = [stat_ref[d] for d in range(SETS)]
    count = sum(e[0:1] for e in each)
    mean = sum(e[0:1] * e[1:2] for e in each) / count
    spread = sum(e[2:3] for e in each)
    for e in each:
        off = e[1:2] - mean
        spread = spread + e[0:1] * off * off
    inv_std = lax.rsqrt(spread / count + 1e-05)
    return count, mean, inv_std


def grad_act_body(cot_ref, wide_ref, out_ref):
    out_ref[0] = lax.dot_general(
        cot_ref[...].reshape(BLOCK, D), wide_ref[...], (((1,), (1,)), ((), ())), preferred_element_type=F32
    )


def grad_body(
    conv_ref, x_ref, ga_ref, par_ref, stat_ref, cot_hbm,
    act_ref, gp_ref, first_ref, last_ref, gw_ref,
    total_ref, acc_ref, mom_ref, cot_ref, sem,
):
    step = pl.program_id(0)

    def fetch(i):
        rows = pl.ds(i * CORES, CORES)
        return pltpu.make_async_copy(cot_hbm.at[rows], cot_ref.at[rows], sem.at[i])

    @pl.when(step == 0)
    def _():
        for i in range(Z):
            fetch(i).start()

    @pl.when(step == 0)
    def _():
        total_ref[...] = jnp.zeros_like(total_ref)
        acc_ref[...] = jnp.zeros_like(acc_ref)
        count, mean, inv_std = moments(stat_ref)
        mom_ref[0:1] = mean
        mom_ref[1:2] = inv_std

    mean, inv_std = mom_ref[0:1], mom_ref[1:2]
    m = mask_rows(x_ref[0, HALO : HALO + BLOCK].astype(F32))
    scale = par_ref[KERNEL : KERNEL + 1]
    shift = par_ref[KERNEL + 1 : KERNEL + 2]
    normed = (conv_ref[0] - mean) * inv_std
    pre = scale * normed + shift
    sig = jax.nn.sigmoid(pre)
    act = (m * pre * sig).astype(BF16)
    for half in range(CORES):
        act_ref[half] = fold(act[half * ROWS : (half + 1) * ROWS].astype(F32)).astype(BF16)
    fetch(step).wait()
    cot = cot_ref[pl.ds(step * CORES, CORES)].reshape(BLOCK, D)
    grad_act = ga_ref[0]
    gp = m * grad_act * sig * (1.0 + pre * (1.0 - sig))
    nm = m * normed
    gp_ref[0] = gp
    lane = lax.broadcasted_iota(jnp.int32, (HALO, LANES), 1)
    for ref, at in ((first_ref, 0), (last_ref, BLOCK - HALO)):
        ref[0, 0] = gp[at : at + HALO].astype(BF16)
        ref[0, 1] = jnp.where(
            lane == MASK_LANE, m[at : at + HALO], nm[at : at + HALO]
        ).astype(BF16)

    acc_ref[0] += jnp.sum((gp * normed).reshape(-1, 8, LANES), axis=0)
    acc_ref[1] += jnp.sum(gp.reshape(-1, 8, LANES), axis=0)
    total_ref[...] += lax.dot_general(
        act, cot, (((0,), (0,)), ((), ())), preferred_element_type=F32
    )

    @pl.when(step == Z - 1)
    def _():
        sums = [jnp.sum(acc_ref[i], axis=0, keepdims=True) for i in range(2)]
        rows = jnp.concatenate(list(parts(sums[0])) + list(parts(sums[1])), axis=0).astype(BF16)
        for d in range(SETS):
            gw_ref[d, :, 0:D] = total_ref[d * OWN : (d + 1) * OWN].astype(BF16)
            gw_ref[d, :, D:WIDE] = rows


def back_body(
    set_ref, gp_ref, conv_ref, x_ref, par_ref, stat_ref, sum_ref, left_ref, right_ref,
    pack_ref, taps_ref, sums_ref,
    gc_ref, xf_ref, prev_ref, next_ref, tap_ref, run_ref,
):
    b = pl.program_id(0)

    @pl.when(b == 0)
    def _():
        count, mean, inv_std = moments(stat_ref)
        each = sum_ref[0, :, D:WIDE].astype(F32)
        for d in range(1, SETS):
            each = each + sum_ref[d, :, D:WIDE].astype(F32)
        scale_sum = each[0:1] + each[1:2] + each[2:3]
        shift_sum = each[3:4] + each[4:5] + each[5:6]
        sums_ref[...] = jnp.concatenate([scale_sum, shift_sum, jnp.zeros((6, LANES), F32)], axis=0)
        run_ref[0:1] = par_ref[KERNEL : KERNEL + 1] * inv_std
        run_ref[1:2] = scale_sum / count
        run_ref[2:3] = shift_sum / count
        run_ref[3:4] = mean
        run_ref[4:5] = inv_std
        tap_ref[...] = jnp.zeros_like(tap_ref)

    gain, by_norm, by_one = run_ref[0:1], run_ref[1:2], run_ref[2:3]
    where_am_i = set_ref[0]

    def outside(ref, at):
        gp = ref[at, 0].astype(F32)
        nm = ref[at, 1].astype(F32)
        return gain * (gp - by_one * mask_rows(nm) - by_norm * nm)

    x = x_ref[0, HALO : HALO + BLOCK].astype(F32)
    xf_ref[...] = x
    prev_ref[...] = lane_rows(x, PREV_LANE)
    next_ref[...] = lane_rows(x, NEXT_LANE)
    gc_ref[0:HALO] = outside(left_ref, jnp.where(where_am_i == 0, jnp.maximum(b - 1, 0), b))
    gc_ref[HALO + BLOCK : SPAN] = outside(
        right_ref, jnp.where(where_am_i == SETS - 1, jnp.minimum(b + 1, Z - 1), b)
    )
    m = mask_rows(x)
    normed = (conv_ref[0] - run_ref[3:4]) * run_ref[4:5]
    gc_ref[HALO : HALO + BLOCK] = gain * (gp_ref[0] - m * (by_one + by_norm * normed))
    pieces = []
    for chunk in range(BLOCK // CHUNK):
        at = slice(chunk * CHUNK, (chunk + 1) * CHUNK)
        before, after, centre = prev_ref[at], next_ref[at], xf_ref[at]
        total = jnp.zeros((CHUNK, LANES), F32)
        for k in range(KERNEL):
            near = near_rows(gc_ref, HALO + chunk * CHUNK, HALF - k, before, after)
            total = total + par_ref[k : k + 1] * near
            tap_ref[k] += jnp.sum((centre * near).reshape(-1, 8, LANES), axis=0)
        pieces.append(total)
    for core in range(CORES):
        half = jnp.concatenate(
            pieces[core * (ROWS // CHUNK) : (core + 1) * (ROWS // CHUNK)], axis=0
        )
        half = half * m[core * ROWS : (core + 1) * ROWS]
        pack_ref[core] = fold(half).astype(BF16)

    @pl.when(b == Z - 1)
    def _():
        taps_ref[...] = jnp.sum(tap_ref[...], axis=1)


def out_body(act_ref, w_ref, out_ref):
    total = jnp.zeros((ROWS, D), F32)
    for at in range(GROUP):
        total = total + jnp.dot(
            unfold(act_ref[at].astype(F32)).astype(BF16)[:, :CHAN], w_ref[at * CHAN : (at + 1) * CHAN], preferred_element_type=F32
        )
    out_ref[...] = total.astype(BF16)


def join_body(back_ref, gh_ref, four_ref):
    width = 4 * CHAN
    permute = one_hot()
    for part in range(Z // 2):
        for i in range(4):
            four_ref[:, i * LANES : (i + 1) * LANES] = unfold(back_ref[4 * part + i].astype(F32)).astype(BF16)
        gh_ref[:, part * width : (part + 1) * width] = lax.dot_general(
            four_ref[...], permute, (((1,), (1,)), ((), ())), preferred_element_type=F32
        ).astype(BF16)


def shape(dims, kind):
    return jax.ShapeDtypeStruct(dims, kind)


def local(hidden_in, segment_ids, frame_mask, dw_kernel, norm_scale, norm_shift, out_weight, cotangent):
    core = lax.axis_index("core")
    here = lax.axis_index(ALL)
    this_set = lax.axis_index(OVER_SETS)

    with jax.named_scope("cotangent_of_group"):
        cot_all = lax.all_gather(cotangent, IN_GROUP)

    with jax.named_scope("prepare"):
        seg = lax.dynamic_slice_in_dim(
            jnp.pad(segment_ids, (HALO, LANES - HALO), constant_values=-1), here * ROWS, 2 * LANES
        )
        row = lambda v: v.reshape(1, -1)
        wp, ext, own, edge = call(
            prep_body,
            (
                shape((SETS, OWN, WIDE), BF16),
                shape((ROWS, LANES), F32),
                shape((ROWS, D), BF16),
                shape((HALO, D), BF16),
            ),
            (core.reshape(1), row(seg), dw_kernel.T, row(norm_scale), row(norm_shift), row(frame_mask), out_weight, hidden_in),
            [
                pltpu.VMEM((LANES, LANES), F32),
                pltpu.VMEM((OWN, KERNEL), F32),
                pltpu.VMEM((1, OWN), F32),
                pltpu.VMEM((1, OWN), F32),
                pltpu.VMEM((1, ROWS), jnp.int32),
                pltpu.VMEM((OWN, D), BF16),
                pltpu.SemaphoreType.DMA((6,)),
            ],
            "prepare",
            limit=64,
            in_specs=[smem(), vmem()] + [hbm()] * 6,
            out_specs=[vmem()] * 4,
        )

    with jax.named_scope("edge_frames"):
        last = Z * SETS * CORES - 1
        pairs = [(i, i + 1) for i in range(1, last, 2)] + [(i + 1, i) for i in range(1, last, 2)]
        halo = lax.ppermute(edge, ALL, pairs)

    with jax.named_scope("rows_and_params"):
        wp = lax.all_to_all(wp, OVER_SETS, 0, 0)

    with jax.named_scope("frames_to_channels"):
        frames = call(
            split_body,
            shape((GROUP, SENT, LANES), BF16),
            (core.reshape(1), own, halo, ext),
            [pltpu.VMEM((SENT, D), BF16), pltpu.VMEM((SENT, LANES), F32)],
            "split",
            limit=64,
            in_specs=[smem(), vmem(), vmem(), vmem()],
            out_specs=vmem(),
        )
        frames, wp = lax.optimization_barrier((frames, wp))
        x = lax.all_to_all(frames, IN_GROUP, 0, 0).reshape(Z, SPAN, LANES)

    whole = lambda *dims: pl.BlockSpec(dims, lambda i: (0,) * len(dims))
    each = lambda *dims: pl.BlockSpec(dims, lambda i: (i,) + (0,) * (len(dims) - 1))

    with jax.named_scope("unpack_rows"):
        par, rows, wide = call(
            rows_body,
            (shape((PART, LANES), F32), shape((CHAN, D), BF16), shape((LANES, D), BF16)),
            (wp,),
            [pltpu.VMEM((LANES, LANES), F32), pltpu.VMEM((LANES, WIDE), F32)],
            "rows",
            limit=24,
            work=2 * 10**9,
            in_specs=[vmem()],
            out_specs=[vmem()] * 3,
        )

    with jax.named_scope("conv"):
        conv, stat = call(
            conv_body,
            (shape((Z, BLOCK, LANES), F32), shape((SETS, 8, LANES), F32)),
            (x, par),
            [
                pltpu.VMEM((SPAN, LANES), F32),
                pltpu.VMEM((BLOCK, LANES), F32),
                pltpu.VMEM((BLOCK, LANES), F32),
                pltpu.VMEM((8, LANES), F32),
            ],
            "conv",
            limit=24,
            work=6 * 10**9,
            grid=(Z,),
            in_specs=[each(1, SPAN, LANES), whole(PART, LANES)],
            out_specs=[each(1, BLOCK, LANES), whole(SETS, 8, LANES)],
        )

    with jax.named_scope("weights_of_group"):
        rows, conv = lax.optimization_barrier((rows, conv))
        w_all = lax.all_gather(rows, IN_GROUP, tiled=True)

    with jax.named_scope("norm_sums"):
        stat = lax.all_to_all(stat, OVER_SETS, 0, 0)

    with jax.named_scope("grad_act"):
        wide, conv = lax.optimization_barrier((wide, conv))
        grad_act = call(
            grad_act_body,
            shape((Z, BLOCK, LANES), F32),
            (cot_all, wide),
            [],
            "grad_act",
            limit=GA,
            work=4 * 10**9,
            grid=(Z,),
            in_specs=[each(CORES, ROWS, D), whole(LANES, D)],
            out_specs=each(1, BLOCK, LANES),
        )

    with jax.named_scope("activation_grad"):
        act, gp, first, last_rows, gw = call(
            grad_body,
            (
                shape((GROUP, CHAN, LANES), BF16),
                shape((Z, BLOCK, LANES), F32),
                shape((Z, 2, HALO, LANES), BF16),
                shape((Z, 2, HALO, LANES), BF16),
                shape((SETS, OWN, WIDE), BF16),
            ),
            (conv, x, grad_act, par, stat, cot_all),
            [
                pltpu.VMEM((LANES, D), F32),
                pltpu.VMEM((2, 8, LANES), F32),
                pltpu.VMEM((8, LANES), F32),
                pltpu.VMEM((GROUP, ROWS, D), BF16),
                pltpu.SemaphoreType.DMA((Z,)),
            ],
            "activation",
            limit=48,
            grid=(Z,),
            in_specs=[
                pl.BlockSpec((1, BLOCK, LANES), lambda i: (i, 0, 0)),
                pl.BlockSpec((1, SPAN, LANES), lambda i: (i, 0, 0)),
                pl.BlockSpec((1, BLOCK, LANES), lambda i: (i, 0, 0)),
                whole(PART, LANES),
                whole(SETS, 8, LANES),
                hbm(),
            ],
            out_specs=[
                pl.BlockSpec((CORES, CHAN, LANES), lambda i: (i, 0, 0)),
                pl.BlockSpec((1, BLOCK, LANES), lambda i: (i, 0, 0)),
                pl.BlockSpec((1, 2, HALO, LANES), lambda i: (i, 0, 0, 0)),
                pl.BlockSpec((1, 2, HALO, LANES), lambda i: (i, 0, 0, 0)),
                whole(SETS, OWN, WIDE),
            ],
        )

    with jax.named_scope("edge_grads"):
        up = [(i, (i + 1) % SETS) for i in range(SETS)]
        down = [((i + 1) % SETS, i) for i in range(SETS)]
        left = lax.ppermute(last_rows, OVER_SETS, up)
        right = lax.ppermute(first, OVER_SETS, down)

    with jax.named_scope("norm_grad_sums"):
        gw = lax.all_to_all(gw, OVER_SETS, 0, 0)

    with jax.named_scope("act_to_frames"):
        act, gw = lax.optimization_barrier((act, gw))
        act = lax.all_to_all(act, IN_GROUP, 0, 0)

    with jax.named_scope("conv_grad"):
        pack, taps, both = call(
            back_body,
            (
                shape((GROUP, CHAN, LANES), BF16),
                shape((32, LANES), F32),
                shape((8, LANES), F32),
            ),
            (this_set.reshape(1), gp, conv, x, par, stat, gw, left, right),
            [
                pltpu.VMEM((SPAN, LANES), F32),
                pltpu.VMEM((BLOCK, LANES), F32),
                pltpu.VMEM((BLOCK, LANES), F32),
                pltpu.VMEM((BLOCK, LANES), F32),
                pltpu.VMEM((32, 8, LANES), F32),
                pltpu.VMEM((8, LANES), F32),
            ],
            "conv_grad",
            limit=24,
            work=10**10,
            grid=(Z,),
            in_specs=[
                smem(),
                each(1, BLOCK, LANES),
                each(1, BLOCK, LANES),
                each(1, SPAN, LANES),
                whole(PART, LANES),
                whole(SETS, 8, LANES),
                whole(SETS, OWN, WIDE),
                whole(Z, 2, HALO, LANES),
                whole(Z, 2, HALO, LANES),
            ],
            out_specs=[each(CORES, CHAN, LANES), whole(32, LANES), whole(8, LANES)],
        )

    with jax.named_scope("channels_to_frames"):
        back = lax.all_to_all(pack, IN_GROUP, 0, 0)

    with jax.named_scope("module_out"):
        taps, w_all, act = lax.optimization_barrier((taps, w_all, act))
        module_out = call(
            out_body,
            shape((ROWS, D), BF16),
            (act, w_all),
            [],
            "module_out",
            limit=24,
            work=4 * 10**9,
            in_specs=[vmem()] * 2,
            out_specs=vmem(),
        )

    with jax.named_scope("sums_of_taps"):
        for axis, size in (("x", X), ("y", Y)):
            moved = [
                lax.ppermute(taps, axis, [(i, (i + by) % size) for i in range(size)])
                for by in range(1, size)
            ]
            *moved, module_out = lax.optimization_barrier((*moved, module_out))
            taps = taps + sum(moved)
        at = this_set * OWN
        grad_kernel = lax.dynamic_slice(taps, (0, at), (KERNEL, OWN))
        grad_scale = lax.dynamic_slice(both, (0, at), (1, OWN))[0]
        grad_shift = lax.dynamic_slice(both, (1, at), (1, OWN))[0]

    with jax.named_scope("weight_grad_sums"):
        grad_weight = jnp.sum(gw[:, :, :D].astype(F32), axis=0)

    with jax.named_scope("join"):
        grad_hidden = call(
            join_body,
            shape((ROWS, D), BF16),
            (back,),
            [pltpu.VMEM((ROWS, 4 * LANES), BF16)],
            "join",
            limit=24,
            in_specs=[vmem()],
            out_specs=vmem(),
        )
    return (module_out, grad_hidden, grad_kernel, grad_scale, grad_shift, grad_weight)


def solution(mesh):
    grid = Mesh(mesh.devices.reshape(Z, X, Y, CORES), ALL)
    return jax.shard_map(
        local,
        mesh=grid,
        in_specs=(P(ALL, None), P(), P(ALL), P(None, ALL), P(ALL), P(ALL), P(ALL, None), P(ALL, None)),
        out_specs=(P(ALL, None), P(ALL, None), P(None, ALL), P(ALL), P(ALL), P(ALL, None)),
        check_vma=False,
    )
```

```python
import jax
import jax.numpy as jnp
from jax import lax
from jax.experimental import pallas as pl
from jax.experimental.pallas import tpu as pltpu
from jax.sharding import Mesh, PartitionSpec as P

Z, X, Y, CORES = 8, 4, 4, 2
GROUP = Z * CORES
SETS = X * Y
KERNEL = 31
HALF = KERNEL // 2
D = 1536
ROWS = 128
OWN = D // (GROUP * SETS)
CHAN = OWN * SETS
HALO = 16
LANES = 128
BLOCK = CORES * ROWS
SPAN = BLOCK + 2 * HALO
SENT = ROWS + HALO
CHUNK = 32
WIDE = D + LANES
PART = 40
GA = 48
MASK_LANE, PREV_LANE, NEXT_LANE = CHAN, CHAN + 1, CHAN + 2
ALL = ("z", "x", "y", "core")
IN_GROUP = ("z", "core")
OVER_SETS = ("x", "y")
F32, BF16 = jnp.float32, jnp.bfloat16


def call(body, outs, ins, scratch, name, limit=64, work=0, **more):
    if work:
        more["cost_estimate"] = pl.CostEstimate(flops=work, bytes_accessed=2**20, transcendentals=0)
    if scratch:
        more["scratch_shapes"] = scratch
    return pl.pallas_call(
        body,
        out_shape=outs,
        name=name,
        compiler_params=pltpu.CompilerParams(vmem_limit_bytes=limit * 2**20),
        **more,
    )(*ins)


def vmem():
    return pl.BlockSpec(memory_space=pltpu.VMEM)


def hbm():
    return pl.BlockSpec(memory_space=pltpu.HBM)


def parts(x):
    high = x.astype(BF16).astype(F32)
    mid = (x - high).astype(BF16).astype(F32)
    return high, mid, (x - high - mid).astype(BF16).astype(F32)


def smem():
    return pl.BlockSpec(memory_space=pltpu.SMEM)


def one_hot():
    col = lax.broadcasted_iota(jnp.int32, (1, 4 * LANES), 1)
    lane = col % LANES
    piece = col // LANES
    source = (
        (piece // 2) * (D // Z) + (lane // OWN) * (CORES * OWN) + (piece % 2) * OWN + lane % OWN
    )
    source = jnp.where(lane < CHAN, source, -1)
    row = lax.broadcasted_iota(jnp.int32, (2 * D // Z, 4 * LANES), 0)
    return jnp.where(row == source, 1.0, 0.0).astype(BF16)


def prep_body(
    core_ref, seg_ref, taps_hbm, scale_hbm, shift_hbm, mask_hbm, w_hbm, own_hbm,
    wp_ref, ext_ref, own_ref, edge_ref,
    tmp_ref, taps_ref, scale_ref, shift_ref, mask_ref, w_ref, sem,
):
    pairs = (
        (taps_hbm, taps_ref), (scale_hbm, scale_ref), (shift_hbm, shift_ref),
        (mask_hbm, mask_ref), (w_hbm, w_ref), (own_hbm, own_ref),
    )
    copies = [pltpu.make_async_copy(a, b, sem.at[i]) for i, (a, b) in enumerate(pairs)]
    for copy in copies:
        copy.start()
    tmp_ref[...] = jnp.zeros_like(tmp_ref)
    for copy in copies:
        copy.wait()
    tmp_ref[KERNEL : KERNEL + 1, 0:OWN] = scale_ref[...]
    tmp_ref[KERNEL + 1 : KERNEL + 2, 0:OWN] = shift_ref[...]
    rows = tmp_ref[...].T
    tmp_ref[0:8] = rows[0:8]
    tmp_ref[0:OWN, 0:KERNEL] = taps_ref[...]
    high, mid, low = parts(tmp_ref[0:8])
    side = high + pltpu.roll(mid, PART, 1) + pltpu.roll(low, 2 * PART, 1)
    side = side[0:OWN].astype(BF16)
    for d in range(SETS):
        wp_ref[d, :, 0:D] = w_ref[...]
        wp_ref[d, :, D:WIDE] = side
    seg = seg_ref[...]
    own = seg[:, HALO : HALO + ROWS]
    before = jnp.zeros((1, ROWS), F32)
    after = jnp.zeros((1, ROWS), F32)
    for j in range(1, HALF + 1):
        before = before + jnp.where(seg[:, HALO - j : HALO - j + ROWS] == own, 1.0, 0.0)
        after = after + jnp.where(seg[:, HALO + j : HALO + j + ROWS] == own, 1.0, 0.0)
    tmp_ref[...] = jnp.zeros_like(tmp_ref)
    tmp_ref[MASK_LANE : MASK_LANE + 1] = mask_ref[...].astype(F32)
    tmp_ref[PREV_LANE : PREV_LANE + 1] = before
    tmp_ref[NEXT_LANE : NEXT_LANE + 1] = after
    ext = tmp_ref[...].T
    ext_ref[...] = ext
    keep = ext[:, MASK_LANE : MASK_LANE + 1] > 0.5
    own = jnp.where(keep, own_ref[...].astype(F32), 0.0).astype(BF16)
    own_ref[...] = own
    edge_ref[...] = jnp.where(core_ref[0] == 0, own[0:HALO].astype(F32), own[ROWS - HALO :].astype(F32)).astype(BF16)


def split_body(core_ref, own_ref, halo_ref, ext_ref, out_ref, rows_ref, side_ref):
    own = own_ref[...]
    none = jnp.zeros((HALO, LANES), F32)

    @pl.when(core_ref[0] == 0)
    def _():
        rows_ref[0:HALO] = halo_ref[...]
        rows_ref[HALO:SENT] = own
        side_ref[0:HALO] = none
        side_ref[HALO:SENT] = ext_ref[...]

    @pl.when(core_ref[0] != 0)
    def _():
        rows_ref[0:ROWS] = own
        rows_ref[ROWS:SENT] = halo_ref[...]
        side_ref[0:ROWS] = ext_ref[...]
        side_ref[ROWS:SENT] = none

    ext = side_ref[...]
    permute = one_hot()
    width = 2 * D // Z
    for part in range(Z // 2):
        piece = rows_ref[:, part * width : (part + 1) * width]
        moved = jnp.dot(piece, permute, preferred_element_type=F32)
        for i in range(4):
            out_ref[4 * part + i] = (moved[:, i * LANES : (i + 1) * LANES] + ext).astype(BF16)


def lane_rows(x, lane):
    return jnp.broadcast_to(x[:, lane : lane + 1], x.shape)


def mask_rows(x):
    return lane_rows(x, MASK_LANE)


def near_rows(ref, base, offset, before, after):
    rows = ref[base + offset : base + offset + CHUNK]
    if offset == 0:
        return rows
    same = before >= -offset if offset < 0 else after >= offset
    return jnp.where(same, rows, 0.0)


def rows_body(wp_ref, par_ref, w_ref, wide_ref, tmp_ref, wf_ref):
    wf_ref[CHAN:] = jnp.zeros((LANES - CHAN, WIDE), F32)
    for d in range(SETS):
        wf_ref[d * OWN : (d + 1) * OWN] = wp_ref[d].astype(F32)
    wide = wf_ref[:, 0:D].astype(BF16)
    wide_ref[...] = wide
    w_ref[...] = wide[:CHAN]
    tmp_ref[...] = wf_ref[:, D:WIDE].T
    par_ref[...] = tmp_ref[0:PART] + tmp_ref[PART : 2 * PART] + tmp_ref[2 * PART : 3 * PART]


def conv_body(
    x_ref, par_ref, conv_ref, stat_ref, xf_ref, prev_ref, next_ref, run_ref
):
    step = pl.program_id(0)

    @pl.when(step == 0)
    def _():
        run_ref[...] = jnp.zeros_like(run_ref)

    x = x_ref[0].astype(F32)
    xf_ref[...] = x
    inside = x[HALO : HALO + BLOCK]
    prev_ref[...] = lane_rows(inside, PREV_LANE)
    next_ref[...] = lane_rows(inside, NEXT_LANE)
    for chunk in range(BLOCK // CHUNK):
        at = slice(chunk * CHUNK, (chunk + 1) * CHUNK)
        before, after = prev_ref[at], next_ref[at]
        total = jnp.zeros((CHUNK, LANES), F32)
        for k in range(KERNEL):
            near = near_rows(xf_ref, HALO + chunk * CHUNK, k - HALF, before, after)
            total = total + par_ref[k : k + 1] * near
        conv_ref[0, at] = total

    rows = lambda v: jnp.sum(jnp.sum(v.reshape(-1, 8, LANES), axis=0), axis=0, keepdims=True)
    m = mask_rows(inside)
    conv = conv_ref[0]
    here = rows(m)
    mean_here = rows(m * conv) / here
    off = conv - mean_here
    count, mean, spread = run_ref[0:1], run_ref[1:2], run_ref[2:3]
    both = count + here
    apart = mean_here - mean
    run_ref[0:1] = both
    run_ref[1:2] = mean + apart * (here / both)
    run_ref[2:3] = spread + rows(m * off * off) + apart * apart * (count * here / both)

    @pl.when(step == Z - 1)
    def _():
        for d in range(SETS):
            stat_ref[d] = run_ref[...]


def fold(x):
    tail = x[CHAN:]
    lane = lax.broadcasted_iota(jnp.int32, tail.shape, 1)
    size = LANES - CHAN
    return jnp.concatenate(
        [
            jnp.where(lane < CHAN, x[g * size : (g + 1) * size], pltpu.roll(tail, CHAN - g * size, 1))
            for g in range(CHAN // size)
        ],
        axis=0,
    )


def unfold(x):
    size = LANES - CHAN
    lane = lax.broadcasted_iota(jnp.int32, (size, LANES), 1)
    tail = jnp.zeros((size, LANES), F32)
    for g in range(CHAN // size):
        turned = pltpu.roll(x[g * size : (g + 1) * size], (g + 1) * size, 1)
        tail = jnp.where((lane >= g * size) & (lane < (g + 1) * size), turned, tail)
    return jnp.concatenate([x, tail], axis=0)


def moments(stat_ref):
    each = [stat_ref[d] for d in range(SETS)]
    count = sum(e[0:1] for e in each)
    mean = sum(e[0:1] * e[1:2] for e in each) / count
    spread = sum(e[2:3] for e in each)
    for e in each:
        off = e[1:2] - mean
        spread = spread + e[0:1] * off * off
    inv_std = lax.rsqrt(spread / count + 1e-05)
    return count, mean, inv_std


def grad_act_body(cot_ref, wide_ref, out_ref):
    out_ref[0] = lax.dot_general(
        cot_ref[...].reshape(BLOCK, D), wide_ref[...], (((1,), (1,)), ((), ())), preferred_element_type=F32
    )


def grad_body(
    conv_ref, x_ref, ga_ref, par_ref, stat_ref, cot_hbm,
    act_ref, gp_ref, first_ref, last_ref, gw_ref,
    total_ref, acc_ref, mom_ref, cot_ref, sem,
):
    step = pl.program_id(0)

    def fetch(i):
        rows = pl.ds(i * CORES, CORES)
        return pltpu.make_async_copy(cot_hbm.at[rows], cot_ref.at[rows], sem.at[i])

    @pl.when(step == 0)
    def _():
        for i in range(Z):
            fetch(i).start()

    @pl.when(step == 0)
    def _():
        total_ref[...] = jnp.zeros_like(total_ref)
        acc_ref[...] = jnp.zeros_like(acc_ref)
        count, mean, inv_std = moments(stat_ref)
        mom_ref[0:1] = mean
        mom_ref[1:2] = inv_std

    mean, inv_std = mom_ref[0:1], mom_ref[1:2]
    m = mask_rows(x_ref[0, HALO : HALO + BLOCK].astype(F32))
    scale = par_ref[KERNEL : KERNEL + 1]
    shift = par_ref[KERNEL + 1 : KERNEL + 2]
    normed = (conv_ref[0] - mean) * inv_std
    pre = scale * normed + shift
    sig = jax.nn.sigmoid(pre)
    act = (m * pre * sig).astype(BF16)
    for half in range(CORES):
        act_ref[half] = fold(act[half * ROWS : (half + 1) * ROWS].astype(F32)).astype(BF16)
    fetch(step).wait()
    cot = cot_ref[pl.ds(step * CORES, CORES)].reshape(BLOCK, D)
    grad_act = ga_ref[0]
    gp = m * grad_act * sig * (1.0 + pre * (1.0 - sig))
    nm = m * normed
    gp_ref[0] = gp
    lane = lax.broadcasted_iota(jnp.int32, (HALO, LANES), 1)
    for ref, at in ((first_ref, 0), (last_ref, BLOCK - HALO)):
        ref[0, 0] = gp[at : at + HALO].astype(BF16)
        ref[0, 1] = jnp.where(
            lane == MASK_LANE, m[at : at + HALO], nm[at : at + HALO]
        ).astype(BF16)

    acc_ref[0] += jnp.sum((gp * normed).reshape(-1, 8, LANES), axis=0)
    acc_ref[1] += jnp.sum(gp.reshape(-1, 8, LANES), axis=0)
    total_ref[...] += lax.dot_general(
        act, cot, (((0,), (0,)), ((), ())), preferred_element_type=F32
    )

    @pl.when(step == Z - 1)
    def _():
        sums = [jnp.sum(acc_ref[i], axis=0, keepdims=True) for i in range(2)]
        rows = jnp.concatenate(list(parts(sums[0])) + list(parts(sums[1])), axis=0).astype(BF16)
        for d in range(SETS):
            gw_ref[d, :, 0:D] = total_ref[d * OWN : (d + 1) * OWN].astype(BF16)
            gw_ref[d, :, D:WIDE] = rows


def back_body(
    set_ref, gp_ref, conv_ref, x_ref, par_ref, stat_ref, sum_ref, left_ref, right_ref,
    pack_ref, taps_ref, sums_ref,
    gc_ref, xf_ref, prev_ref, next_ref, tap_ref, run_ref,
):
    b = pl.program_id(0)

    @pl.when(b == 0)
    def _():
        count, mean, inv_std = moments(stat_ref)
        each = sum_ref[0, :, D:WIDE].astype(F32)
        for d in range(1, SETS):
            each = each + sum_ref[d, :, D:WIDE].astype(F32)
        scale_sum = each[0:1] + each[1:2] + each[2:3]
        shift_sum = each[3:4] + each[4:5] + each[5:6]
        sums_ref[...] = jnp.concatenate([scale_sum, shift_sum, jnp.zeros((6, LANES), F32)], axis=0)
        run_ref[0:1] = par_ref[KERNEL : KERNEL + 1] * inv_std
        run_ref[1:2] = scale_sum / count
        run_ref[2:3] = shift_sum / count
        run_ref[3:4] = mean
        run_ref[4:5] = inv_std
        tap_ref[...] = jnp.zeros_like(tap_ref)

    gain, by_norm, by_one = run_ref[0:1], run_ref[1:2], run_ref[2:3]
    where_am_i = set_ref[0]

    def outside(ref, at):
        gp = ref[at, 0].astype(F32)
        nm = ref[at, 1].astype(F32)
        return gain * (gp - by_one * mask_rows(nm) - by_norm * nm)

    x = x_ref[0, HALO : HALO + BLOCK].astype(F32)
    xf_ref[...] = x
    prev_ref[...] = lane_rows(x, PREV_LANE)
    next_ref[...] = lane_rows(x, NEXT_LANE)
    gc_ref[0:HALO] = outside(left_ref, jnp.where(where_am_i == 0, jnp.maximum(b - 1, 0), b))
    gc_ref[HALO + BLOCK : SPAN] = outside(
        right_ref, jnp.where(where_am_i == SETS - 1, jnp.minimum(b + 1, Z - 1), b)
    )
    m = mask_rows(x)
    normed = (conv_ref[0] - run_ref[3:4]) * run_ref[4:5]
    gc_ref[HALO : HALO + BLOCK] = gain * (gp_ref[0] - m * (by_one + by_norm * normed))
    pieces = []
    for chunk in range(BLOCK // CHUNK):
        at = slice(chunk * CHUNK, (chunk + 1) * CHUNK)
        before, after, centre = prev_ref[at], next_ref[at], xf_ref[at]
        total = jnp.zeros((CHUNK, LANES), F32)
        for k in range(KERNEL):
            near = near_rows(gc_ref, HALO + chunk * CHUNK, HALF - k, before, after)
            total = total + par_ref[k : k + 1] * near
            tap_ref[k] += jnp.sum((centre * near).reshape(-1, 8, LANES), axis=0)
        pieces.append(total)
    for core in range(CORES):
        half = jnp.concatenate(
            pieces[core * (ROWS // CHUNK) : (core + 1) * (ROWS // CHUNK)], axis=0
        )
        half = half * m[core * ROWS : (core + 1) * ROWS]
        pack_ref[core] = fold(half).astype(BF16)

    @pl.when(b == Z - 1)
    def _():
        taps_ref[...] = jnp.sum(tap_ref[...], axis=1)


def out_body(act_ref, w_ref, out_ref):
    total = jnp.zeros((ROWS, D), F32)
    for at in range(GROUP):
        total = total + jnp.dot(
            unfold(act_ref[at].astype(F32)).astype(BF16)[:, :CHAN], w_ref[at * CHAN : (at + 1) * CHAN], preferred_element_type=F32
        )
    out_ref[...] = total.astype(BF16)


def join_body(back_ref, gh_ref, four_ref):
    width = 4 * CHAN
    permute = one_hot()
    for part in range(Z // 2):
        for i in range(4):
            four_ref[:, i * LANES : (i + 1) * LANES] = unfold(back_ref[4 * part + i].astype(F32)).astype(BF16)
        gh_ref[:, part * width : (part + 1) * width] = lax.dot_general(
            four_ref[...], permute, (((1,), (1,)), ((), ())), preferred_element_type=F32
        ).astype(BF16)


def shape(dims, kind):
    return jax.ShapeDtypeStruct(dims, kind)


def local(hidden_in, segment_ids, frame_mask, dw_kernel, norm_scale, norm_shift, out_weight, cotangent):
    core = lax.axis_index("core")
    here = lax.axis_index(ALL)
    this_set = lax.axis_index(OVER_SETS)

    with jax.named_scope("cotangent_of_group"):
        cot_all = lax.all_gather(cotangent, IN_GROUP)

    with jax.named_scope("prepare"):
        seg = lax.dynamic_slice_in_dim(
            jnp.pad(segment_ids, (HALO, LANES - HALO), constant_values=-1), here * ROWS, 2 * LANES
        )
        row = lambda v: v.reshape(1, -1)
        wp, ext, own, edge = call(
            prep_body,
            (
                shape((SETS, OWN, WIDE), BF16),
                shape((ROWS, LANES), F32),
                shape((ROWS, D), BF16),
                shape((HALO, D), BF16),
            ),
            (core.reshape(1), row(seg), dw_kernel.T, row(norm_scale), row(norm_shift), row(frame_mask), out_weight, hidden_in),
            [
                pltpu.VMEM((LANES, LANES), F32),
                pltpu.VMEM((OWN, KERNEL), F32),
                pltpu.VMEM((1, OWN), F32),
                pltpu.VMEM((1, OWN), F32),
                pltpu.VMEM((1, ROWS), jnp.int32),
                pltpu.VMEM((OWN, D), BF16),
                pltpu.SemaphoreType.DMA((6,)),
            ],
            "prepare",
            limit=64,
            in_specs=[smem(), vmem()] + [hbm()] * 6,
            out_specs=[vmem()] * 4,
        )

    with jax.named_scope("edge_frames"):
        last = Z * SETS * CORES - 1
        pairs = [(i, i + 1) for i in range(1, last, 2)] + [(i + 1, i) for i in range(1, last, 2)]
        halo = lax.ppermute(edge, ALL, pairs)

    with jax.named_scope("rows_and_params"):
        wp = lax.all_to_all(wp, OVER_SETS, 0, 0)

    with jax.named_scope("frames_to_channels"):
        frames = call(
            split_body,
            shape((GROUP, SENT, LANES), BF16),
            (core.reshape(1), own, halo, ext),
            [pltpu.VMEM((SENT, D), BF16), pltpu.VMEM((SENT, LANES), F32)],
            "split",
            limit=64,
            in_specs=[smem(), vmem(), vmem(), vmem()],
            out_specs=vmem(),
        )
        frames, wp = lax.optimization_barrier((frames, wp))
        x = lax.all_to_all(frames, IN_GROUP, 0, 0).reshape(Z, SPAN, LANES)

    whole = lambda *dims: pl.BlockSpec(dims, lambda i: (0,) * len(dims))
    each = lambda *dims: pl.BlockSpec(dims, lambda i: (i,) + (0,) * (len(dims) - 1))

    with jax.named_scope("unpack_rows"):
        par, rows, wide = call(
            rows_body,
            (shape((PART, LANES), F32), shape((CHAN, D), BF16), shape((LANES, D), BF16)),
            (wp,),
            [pltpu.VMEM((LANES, LANES), F32), pltpu.VMEM((LANES, WIDE), F32)],
            "rows",
            limit=24,
            work=2 * 10**9,
            in_specs=[vmem()],
            out_specs=[vmem()] * 3,
        )

    with jax.named_scope("conv"):
        conv, stat = call(
            conv_body,
            (shape((Z, BLOCK, LANES), F32), shape((SETS, 8, LANES), F32)),
            (x, par),
            [
                pltpu.VMEM((SPAN, LANES), F32),
                pltpu.VMEM((BLOCK, LANES), F32),
                pltpu.VMEM((BLOCK, LANES), F32),
                pltpu.VMEM((8, LANES), F32),
            ],
            "conv",
            limit=24,
            work=6 * 10**9,
            grid=(Z,),
            in_specs=[each(1, SPAN, LANES), whole(PART, LANES)],
            out_specs=[each(1, BLOCK, LANES), whole(SETS, 8, LANES)],
        )

    with jax.named_scope("weights_of_group"):
        rows, conv = lax.optimization_barrier((rows, conv))
        w_all = lax.all_gather(rows, IN_GROUP, tiled=True)

    with jax.named_scope("norm_sums"):
        stat = lax.all_to_all(stat, OVER_SETS, 0, 0)

    with jax.named_scope("grad_act"):
        wide, conv = lax.optimization_barrier((wide, conv))
        grad_act = call(
            grad_act_body,
            shape((Z, BLOCK, LANES), F32),
            (cot_all, wide),
            [],
            "grad_act",
            limit=GA,
            work=4 * 10**9,
            grid=(Z,),
            in_specs=[each(CORES, ROWS, D), whole(LANES, D)],
            out_specs=each(1, BLOCK, LANES),
        )

    with jax.named_scope("activation_grad"):
        act, gp, first, last_rows, gw = call(
            grad_body,
            (
                shape((GROUP, CHAN, LANES), BF16),
                shape((Z, BLOCK, LANES), F32),
                shape((Z, 2, HALO, LANES), BF16),
                shape((Z, 2, HALO, LANES), BF16),
                shape((SETS, OWN, WIDE), BF16),
            ),
            (conv, x, grad_act, par, stat, cot_all),
            [
                pltpu.VMEM((LANES, D), F32),
                pltpu.VMEM((2, 8, LANES), F32),
                pltpu.VMEM((8, LANES), F32),
                pltpu.VMEM((GROUP, ROWS, D), BF16),
                pltpu.SemaphoreType.DMA((Z,)),
            ],
            "activation",
            limit=48,
            grid=(Z,),
            in_specs=[
                pl.BlockSpec((1, BLOCK, LANES), lambda i: (i, 0, 0)),
                pl.BlockSpec((1, SPAN, LANES), lambda i: (i, 0, 0)),
                pl.BlockSpec((1, BLOCK, LANES), lambda i: (i, 0, 0)),
                whole(PART, LANES),
                whole(SETS, 8, LANES),
                hbm(),
            ],
            out_specs=[
                pl.BlockSpec((CORES, CHAN, LANES), lambda i: (i, 0, 0)),
                pl.BlockSpec((1, BLOCK, LANES), lambda i: (i, 0, 0)),
                pl.BlockSpec((1, 2, HALO, LANES), lambda i: (i, 0, 0, 0)),
                pl.BlockSpec((1, 2, HALO, LANES), lambda i: (i, 0, 0, 0)),
                whole(SETS, OWN, WIDE),
            ],
        )

    with jax.named_scope("edge_grads"):
        up = [(i, (i + 1) % SETS) for i in range(SETS)]
        down = [((i + 1) % SETS, i) for i in range(SETS)]
        left = lax.ppermute(last_rows, OVER_SETS, up)
        right = lax.ppermute(first, OVER_SETS, down)

    with jax.named_scope("norm_grad_sums"):
        gw = lax.all_to_all(gw, OVER_SETS, 0, 0)

    with jax.named_scope("act_to_frames"):
        act, gw = lax.optimization_barrier((act, gw))
        act = lax.all_to_all(act, IN_GROUP, 0, 0)

    with jax.named_scope("conv_grad"):
        pack, taps, both = call(
            back_body,
            (
                shape((GROUP, CHAN, LANES), BF16),
                shape((32, LANES), F32),
                shape((8, LANES), F32),
            ),
            (this_set.reshape(1), gp, conv, x, par, stat, gw, left, right),
            [
                pltpu.VMEM((SPAN, LANES), F32),
                pltpu.VMEM((BLOCK, LANES), F32),
                pltpu.VMEM((BLOCK, LANES), F32),
                pltpu.VMEM((BLOCK, LANES), F32),
                pltpu.VMEM((32, 8, LANES), F32),
                pltpu.VMEM((8, LANES), F32),
            ],
            "conv_grad",
            limit=24,
            work=10**10,
            grid=(Z,),
            in_specs=[
                smem(),
                each(1, BLOCK, LANES),
                each(1, BLOCK, LANES),
                each(1, SPAN, LANES),
                whole(PART, LANES),
                whole(SETS, 8, LANES),
                whole(SETS, OWN, WIDE),
                whole(Z, 2, HALO, LANES),
                whole(Z, 2, HALO, LANES),
            ],
            out_specs=[each(CORES, CHAN, LANES), whole(32, LANES), whole(8, LANES)],
        )

    with jax.named_scope("channels_to_frames"):
        back = lax.all_to_all(pack, IN_GROUP, 0, 0)

    with jax.named_scope("module_out"):
        taps, w_all, act = lax.optimization_barrier((taps, w_all, act))
        module_out = call(
            out_body,
            shape((ROWS, D), BF16),
            (act, w_all),
            [],
            "module_out",
            limit=24,
            work=4 * 10**9,
            in_specs=[vmem()] * 2,
            out_specs=vmem(),
        )

    with jax.named_scope("sums_of_taps"):
        for axis, size in (("x", X), ("y", Y)):
            moved = [
                lax.ppermute(taps, axis, [(i, (i + by) % size) for i in range(size)])
                for by in range(1, size)
            ]
            *moved, module_out = lax.optimization_barrier((*moved, module_out))
            taps = taps + sum(moved)
        at = this_set * OWN
        grad_kernel = lax.dynamic_slice(taps, (0, at), (KERNEL, OWN))
        grad_scale = lax.dynamic_slice(both, (0, at), (1, OWN))[0]
        grad_shift = lax.dynamic_slice(both, (1, at), (1, OWN))[0]

    with jax.named_scope("weight_grad_sums"):
        grad_weight = jnp.sum(gw[:, :, :D].astype(F32), axis=0)

    with jax.named_scope("join"):
        grad_hidden = call(
            join_body,
            shape((ROWS, D), BF16),
            (back,),
            [pltpu.VMEM((ROWS, 4 * LANES), BF16)],
            "join",
            limit=24,
            in_specs=[vmem()],
            out_specs=vmem(),
        )
    return (module_out, grad_hidden, grad_kernel, grad_scale, grad_shift, grad_weight)


def solution(mesh):
    grid = Mesh(mesh.devices.reshape(Z, X, Y, CORES), ALL)
    return jax.shard_map(
        local,
        mesh=grid,
        in_specs=(P(ALL, None), P(), P(ALL), P(None, ALL), P(ALL), P(ALL), P(ALL, None), P(ALL, None)),
        out_specs=(P(ALL, None), P(ALL, None), P(None, ALL), P(ALL), P(ALL), P(ALL, None)),
        check_vma=False,
    )
```
